512 devices in a mesh: seq: 64 (over x, y, core), fsdp: 4 (over z_hi), dp: 2 (over z_lo).
Axes of the slice: x: 4, y: 8, z: 8 (z_hi: 4, z_lo: 2; z = z_hi * 2 + z_lo), core: 2. Of those that a mesh axis runs over, the one named last changes fastest.
Arguments:
- qkv: bfloat16 [16384, 3, 4096], P(('dp', 'seq'), None, 'fsdp'), parts along dimension 0, may hold values from -6 to 6
- short_taps: float32 [3, 3, 4096], P(None, None, 'fsdp'), may hold values from -3 to 3
- lifetime: float32 [256, 16], P('fsdp'), may hold values from 30 to 163840
- residues: float32 [256, 16], P('fsdp'), may hold values from -1.5 to 1.5
- skip_gain: float32 [4096], P('fsdp'), may hold values from -4 to 4
- segment_starts: int32 [16], P('dp'), parts along dimension 0, may hold values from 0 to 8191, as said below
- out_weight: bfloat16 [4096, 4096], P('seq', 'fsdp'), may hold values from -0.09375 to 0.09375
Outputs:
- mixed: bfloat16 [16384, 4096], P(('dp', 'seq'), 'fsdp'), parts along dimension 0
The draws below stay inside these ranges and needn't reach their ends.
There are 2 independent parts, one for each index of `dp`. The reference program is written for one: setup_inputs(seed, part) draws one part's arguments, and reference() takes and returns one part's arrays. A program takes and returns all parts, laid end to end along the dimension named above; an argument that names none is the same for every part. Nothing has to cross between parts.
Inputs may be any that keep to these rules, and one draw needn't show every extreme that they name: segment_starts[0] = 0 and the entries rise strictly; document j holds the positions from segment_starts[j] up to the next start (the last one up to 8191).
All inputs are finite; a program needn't handle non-finite values.
Results may differ from the reference program's by a relative error of at most 0.0049.
Values may be sent and summed in bfloat16 or wider, within the bound.
No kernel may reach another device: no remote copies, remote signals or barrier semaphores. Data moves between devices by JAX's collectives and lax.ppermute only.
A program may use at most 128 MiB of HBM per device.

```python
import math
import jax
import jax.numpy as jnp
from jax import lax

D = 4096
GROUP = 16
MODES = 16
SHORT = 3
SEGMENTS = 8
TOKENS = 8192


def draw_segment_starts(key, part):
    key = jax.random.fold_in(key, 5)
    cuts = jax.random.choice(key, TOKENS - 1, (SEGMENTS - 1,), replace=False) + 1
    cuts = jnp.sort(cuts.astype(jnp.int32))
    return jnp.concatenate([jnp.zeros((1,), jnp.int32), cuts])


def draw_lifetime(key, part):
    key = jax.random.fold_in(key, 9)
    first_key = jax.random.fold_in(key, 0)
    shape = (D // GROUP, MODES)
    return jnp.exp(jax.random.uniform(first_key, shape, jnp.float32, math.log(30.0), math.log(10 * TOKENS)))


def shard_levels(key, shape, cuts, smallest, high):
    def one(dim, blocks):
        draws = jax.random.uniform(jax.random.fold_in(jax.random.fold_in(key, 6), dim), (blocks,), jnp.float32, smallest / len(cuts), high / len(cuts))
        return jnp.repeat(jnp.exp(draws), shape[dim] // blocks).reshape((-1,) + (1,) * (len(shape) - dim - 1))

    loudness = one(*cuts[0])
    for cut in cuts[1:]:
        loudness = loudness * one(*cut)
    return loudness


def bell_draw(rng, dims, width, limit, cuts=(), held_as=jnp.bfloat16):
    loudness = shard_levels(rng, dims, cuts, -0.22, 0.18) if cuts else 1.0
    result = jax.random.normal(rng, dims, jnp.float32) * width * loudness
    return jnp.minimum(jnp.maximum(result, -limit), limit).astype(held_as)


def setup_inputs(seed: int = 0, part: int = 0) -> dict:
    key_list = jax.random.split(jax.random.key(seed), 8)
    part_keys = jax.random.split(jax.random.fold_in(key_list[7], part), 8)
    return {
        "qkv": bell_draw(part_keys[0], (TOKENS, 3, D), 1.0, 6.0, ((0, 64), (2, 4))),
        "short_taps": bell_draw(key_list[1], (SHORT, 3, D), 0.6, 3.0, ((2, 4),), jnp.float32),
        "lifetime": draw_lifetime(jax.random.fold_in(key_list[7], 71), part),
        "residues": bell_draw(key_list[3], (D // GROUP, MODES), 0.25, 1.5, ((0, 4),), jnp.float32),
        "skip_gain": bell_draw(key_list[4], (D,), 1.0, 4.0, ((0, 4),), jnp.float32),
        "segment_starts": draw_segment_starts(jax.random.fold_in(jax.random.fold_in(key_list[7], part), 71), part),
        "out_weight": bell_draw(key_list[6], (D, D), D ** -0.5, 0.09375, ((0, 64), (1, 4))),
    }


def segment_of(positions, starts):
    return lax.optimization_barrier(jnp.sum((positions[:, None] >= starts[None, 1:]).astype(jnp.int32), axis=1)).astype(jnp.int32)

def modal_terms(lifetime, residues, block_len):
    decay_rate = 1.0 / lifetime
    weighted = residues * jnp.sqrt(-jnp.expm1(-2.0 * decay_rate))
    offsets = jnp.arange(block_len).astype(jnp.float32)
    falling = jnp.exp(-decay_rate[:, :, None] * offsets[None, None, :])
    rising = jnp.exp(decay_rate[:, :, None] * offsets[None, None, :])
    kernel = jnp.einsum('gmt,gms->gts', weighted[:, :, None] * falling, rising, precision=lax.Precision.HIGHEST)
    entering = weighted[:, :, None] * jnp.exp(-decay_rate[:, :, None] * (offsets[None, None, :] + 1.0))
    leaving = jnp.exp(-decay_rate[:, :, None] * (block_len - 1.0 - offsets[None, None, :]))
    whole_gate = jnp.exp(-decay_rate * block_len)
    causal = (offsets[:, None] >= offsets[None, :]).astype(jnp.float32)
    return (kernel, entering, leaving, whole_gate, causal)

def block_local(kernel, leaving, whole_gate, causal, block_ids, block_vals, prev_id):
    linked = (block_ids[:, None] == block_ids[None, :]).astype(jnp.float32) * causal
    local = jnp.einsum('gts,gcs->gct', kernel * linked[None], block_vals, precision=lax.Precision.HIGHEST)
    closing = (block_ids == block_ids[-1]).astype(jnp.float32)
    fresh = jnp.einsum('gms,gcs->gmc', leaving * closing[None, None, :], block_vals, precision=lax.Precision.HIGHEST)
    gate = whole_gate * (block_ids[-1] == prev_id).astype(jnp.float32)
    return (local, gate, fresh)

def block_carry(entering, block_ids, prev_id, state):
    joined = (block_ids == prev_id).astype(jnp.float32)
    return jnp.einsum('gmt,gmc->gct', entering * joined[None, None, :], state, precision=lax.Precision.HIGHEST)

def reference(qkv, short_taps, lifetime, residues, skip_gain, segment_starts, out_weight):
    positions = jnp.arange(TOKENS).astype(jnp.int32)
    seg_ids = segment_of(positions, segment_starts)
    values_all = qkv.astype(jnp.float32)
    feats = jnp.zeros(values_all.shape, jnp.float32)
    for offset in range(SHORT):
        shifted = jnp.pad(values_all, ((offset, 0), (0, 0), (0, 0)))[:TOKENS]
        earlier_ids = jnp.pad(seg_ids, (offset, 0), constant_values=-1)[:TOKENS]
        same_doc = (earlier_ids == seg_ids).astype(jnp.float32)
        feats = feats + short_taps[offset][None] * shifted * same_doc[:, None, None]
    query = feats[:, 0, :]
    product = feats[:, 1, :] * feats[:, 2, :]
    groups = D // GROUP
    block_len = 128 if TOKENS % 128 == 0 else TOKENS
    kernel, entering, leaving, whole_gate, causal = modal_terms(lifetime, residues, block_len)
    blocks_vals = product.reshape(TOKENS // block_len, block_len, groups, GROUP).transpose(0, 2, 3, 1)
    blocks_ids = seg_ids.reshape(TOKENS // block_len, block_len)

    def advance(carry, inputs):
        state, prev_id = carry
        block_vals, block_ids = inputs
        local, gate, fresh = block_local(kernel, leaving, whole_gate, causal, block_ids, block_vals, prev_id)
        carried = block_carry(entering, block_ids, prev_id, state)
        state = gate[:, :, None] * state + fresh
        return ((state, block_ids[-1].astype(jnp.int32)), local + carried)
    start_state = (jnp.zeros((groups, MODES, GROUP), jnp.float32), jnp.array(-1, jnp.int32))
    _, long_blocks = lax.scan(advance, start_state, (blocks_vals, blocks_ids))
    long_range = long_blocks.transpose(0, 3, 1, 2).reshape(TOKENS, D)
    gated = (query * (long_range + skip_gain[None, :] * product)).astype(jnp.bfloat16)
    return jnp.dot(gated, out_weight, preferred_element_type=jnp.float32).astype(jnp.bfloat16)
```

```python
import jax
import jax.numpy as jnp
from jax import lax
from jax.experimental import pallas as pl
from jax.experimental.pallas import tpu as pltpu
from jax.sharding import PartitionSpec as P

GROUP = 16
MODES = 16
SHORT = 3
LANES = 128
PER_TILE = LANES // GROUP
F32 = jnp.float32
BF16 = jnp.bfloat16
ROOMY = pltpu.CompilerParams(vmem_limit_bytes=48 * 1024 * 1024)
SMEM = pl.BlockSpec(memory_space=pltpu.SMEM)
VMEM = pl.BlockSpec(memory_space=pltpu.VMEM)


def iota(shape, axis):
    return lax.broadcasted_iota(jnp.int32, shape, axis)


def segment_of(starts, positions):
    total = jnp.zeros(positions.shape, jnp.int32)
    for j in range(1, starts.shape[0]):
        total = total + (positions >= starts[j]).astype(jnp.int32)
    return total


def not_start(starts, positions):
    clear = jnp.ones(positions.shape, F32)
    for j in range(starts.shape[0]):
        clear = jnp.where(positions == starts[j], 0.0, clear)
    return clear


def halves(x):
    high = x.astype(BF16)
    return high, (x - high.astype(F32)).astype(BF16)


def split_dot(left, right):
    high, low = halves(right)
    upper = jnp.concatenate([high, low], axis=1)
    lower = jnp.concatenate([high, jnp.zeros_like(low)], axis=1)
    both = jnp.concatenate([upper, lower], axis=0)
    out = jnp.dot(left, both, preferred_element_type=F32)
    return out[:, :LANES] + out[:, LANES:]


def own_group():
    return (iota((PER_TILE, LANES), 0) == iota((PER_TILE, LANES), 1) // GROUP).astype(F32)


def prepare_kernel(starts, lifetime, residues, toeplitz, leaving, entering, decay):
    tile = pl.program_id(0)
    first = lax.axis_index("seq") * LANES
    rows = iota((LANES, LANES), 0)
    cols = iota((LANES, LANES), 1)
    seg_row = segment_of(starts, first + rows)
    seg_col = segment_of(starts, first + cols)
    linked = ((seg_row == seg_col) & (rows >= cols)).astype(F32)
    lane = iota((PER_TILE, LANES), 1)
    seg_lane = segment_of(starts, first + lane)
    last = segment_of(starts, jnp.full((PER_TILE, LANES), first + (LANES - 1)))
    before = jnp.where(first > 0, segment_of(starts, jnp.full((PER_TILE, LANES), first - 1)), -1)
    closing = (seg_lane == last).astype(F32)
    joined = (seg_lane == before).astype(F32)
    offset = lane.astype(F32)
    apart = jnp.where(lane == 0, 0, LANES - lane).astype(F32)
    own = own_group()

    rate = 1.0 / lifetime[...]
    double = 2.0 * rate
    series = double * (
        1.0
        - double
        * (0.5 - double * (1.0 / 6 - double * (1.0 / 24 - double * (1.0 / 120 - double * (1.0 / 720)))))
    )
    weight = residues[...] * jnp.sqrt(jnp.where(double < 0.07, series, 1.0 - jnp.exp(-double)))
    taps = jnp.zeros((PER_TILE, LANES), F32)
    leave_rows = []
    enter_rows = []
    for mode in range(MODES):
        r = jnp.broadcast_to(rate[:, mode : mode + 1], (PER_TILE, LANES))
        w = jnp.broadcast_to(weight[:, mode : mode + 1], (PER_TILE, LANES))
        taps = taps + w * jnp.exp(-r * apart)
        leave_rows.append(jnp.exp(-r * (LANES - 1.0 - offset)) * closing)
        enter_rows.append(w * jnp.exp(-r * (offset + 1.0)) * joined)
        whole = jnp.sum(jnp.exp(-r * LANES) * own, axis=0, keepdims=True)
        decay[4 * mode + tile // 2, pl.ds(tile % 2, 1), :] = whole
    high, low = halves(jnp.concatenate(leave_rows, axis=0))
    leaving[0, :, :LANES] = high
    leaving[0, :, LANES:] = low
    high, low = halves(jnp.concatenate(enter_rows, axis=0).T)
    entering[0, :, :LANES] = high
    entering[0, :, LANES:] = low
    for group in range(PER_TILE):
        spread = jnp.broadcast_to(taps[group : group + 1, :], (LANES, LANES))
        rolled = pltpu.roll(spread, 0, 1, stride=1, stride_axis=0)
        high, low = halves(rolled * linked)
        toeplitz[group, :, :LANES] = high
        toeplitz[group, :, LANES:] = low


def prepare(starts, lifetime, residues):
    tiles = lifetime.shape[0] // PER_TILE
    return pl.pallas_call(
        prepare_kernel,
        grid=(tiles,),
        in_specs=[
            SMEM,
            pl.BlockSpec((PER_TILE, MODES), lambda k: (k, 0)),
            pl.BlockSpec((PER_TILE, MODES), lambda k: (k, 0)),
        ],
        out_specs=[
            pl.BlockSpec((PER_TILE, LANES, 2 * LANES), lambda k: (k, 0, 0)),
            pl.BlockSpec((1, LANES, 2 * LANES), lambda k: (k, 0, 0)),
            pl.BlockSpec((1, LANES, 2 * LANES), lambda k: (k, 0, 0)),
            pl.BlockSpec((8 * tiles, 2, LANES), lambda k: (0, 0, 0)),
        ],
        out_shape=[
            jax.ShapeDtypeStruct((tiles * PER_TILE, LANES, 2 * LANES), BF16),
            jax.ShapeDtypeStruct((tiles, LANES, 2 * LANES), BF16),
            jax.ShapeDtypeStruct((tiles, LANES, 2 * LANES), BF16),
            jax.ShapeDtypeStruct((8 * tiles, 2, LANES), F32),
        ],
        compiler_params=ROOMY,
        name="prepare",
    )(starts, lifetime, residues)


def features_kernel(starts, qkv, rim, taps, leaving, query, product, fresh):
    tile = pl.program_id(0)
    first = lax.axis_index("seq") * LANES
    row = iota((LANES, LANES), 0)
    clear = not_start(starts, first + row)
    clear_before = clear * not_start(starts, first + row - 1)
    feats = []
    for kind in range(3):
        now = qkv[kind].astype(F32)
        edge = rim[kind].astype(F32)
        one = jnp.where(row == 0, edge[1:2, :], pltpu.roll(now, 1, 0))
        two = jnp.where(row == 0, edge[0:1, :], jnp.where(row == 1, edge[1:2, :], pltpu.roll(now, 2, 0)))
        feats.append(
            taps[0, kind : kind + 1, :] * now
            + taps[1, kind : kind + 1, :] * one * clear
            + taps[2, kind : kind + 1, :] * two * clear_before
        )
    query[...] = feats[0]
    values = feats[1] * feats[2]
    product[...] = values
    states = split_dot(leaving[0], values)
    own = own_group()
    for mode in range(MODES):
        some = states[mode * PER_TILE : (mode + 1) * PER_TILE, :] * own
        fresh[4 * mode + tile // 2, pl.ds(tile % 2, 1), :] = jnp.sum(some, axis=0, keepdims=True)


def features(starts, qkv, rim, taps, leaving):
    chans = qkv.shape[2]
    tiles = chans // LANES
    flat = pl.BlockSpec((LANES, LANES), lambda k: (0, k))
    return pl.pallas_call(
        features_kernel,
        grid=(tiles,),
        in_specs=[
            SMEM,
            pl.BlockSpec((3, LANES, LANES), lambda k: (0, 0, k)),
            pl.BlockSpec((3, SHORT - 1, LANES), lambda k: (0, 0, k)),
            pl.BlockSpec((SHORT, 3, LANES), lambda k: (0, 0, k)),
            pl.BlockSpec((1, LANES, 2 * LANES), lambda k: (k, 0, 0)),
        ],
        out_specs=[flat, flat, pl.BlockSpec((8 * tiles, 2, LANES), lambda k: (0, 0, 0))],
        out_shape=[
            jax.ShapeDtypeStruct((LANES, chans), F32),
            jax.ShapeDtypeStruct((LANES, chans), F32),
            jax.ShapeDtypeStruct((8 * tiles, 2, LANES), F32),
        ],
        compiler_params=ROOMY,
        name="features",
    )(starts, qkv, rim, taps, leaving)


def scan_kernel(starts, fresh, decay, entering):
    blocks = fresh.shape[0]
    whole = decay[lax.axis_index("seq")]
    gate = jnp.ones((blocks, 2, LANES), F32)
    number = iota((blocks, 2, LANES), 0)
    for j in range(1, starts.shape[0]):
        gate = jnp.where(number == starts[j] // LANES, 0.0, gate)
    state = jnp.zeros((2, LANES), F32)
    for block in range(blocks):
        entering[block] = state
        state = state * (whole * gate[block]) + fresh[block]


def scan_blocks(starts, fresh, decay):
    return pl.pallas_call(
        scan_kernel,
        in_specs=[SMEM, VMEM, VMEM],
        out_specs=VMEM,
        out_shape=jax.ShapeDtypeStruct(fresh.shape, F32),
        name="scan_blocks",
    )(starts, fresh, decay)


def gate_kernel(toeplitz, entering, query, product, skip, states, gated):
    tile = pl.program_id(0)
    values = product[...]
    lane_group = iota((LANES, LANES), 1) // GROUP
    own = own_group()
    spread = []
    for mode in range(MODES):
        state = states[4 * mode + tile // 2, pl.ds(tile % 2, 1), :]
        spread.append(jnp.broadcast_to(state, (PER_TILE, LANES)) * own)
    total = split_dot(entering[0], jnp.concatenate(spread, axis=0))
    high, low = halves(values)
    upper = jnp.concatenate([high, low], axis=1)
    lower = jnp.concatenate([high, jnp.zeros_like(low)], axis=1)
    both = jnp.concatenate([upper, lower], axis=0)
    local = jnp.zeros((LANES, LANES), F32)
    for group in range(PER_TILE):
        out = jnp.dot(toeplitz[group], both, preferred_element_type=F32)
        local = jnp.where(lane_group == group, out[:, :LANES] + out[:, LANES:], local)
    gated[...] = (query[...] * (local + total + skip[...] * values)).astype(BF16)


def gate(toeplitz, entering, query, product, skip, states):
    chans = query.shape[1]
    flat = pl.BlockSpec((LANES, LANES), lambda k: (0, k))
    return pl.pallas_call(
        gate_kernel,
        grid=(chans // LANES,),
        in_specs=[
            pl.BlockSpec((PER_TILE, LANES, 2 * LANES), lambda k: (k, 0, 0)),
            pl.BlockSpec((1, LANES, 2 * LANES), lambda k: (k, 0, 0)),
            flat,
            flat,
            pl.BlockSpec((1, LANES), lambda k: (0, k)),
            VMEM,
        ],
        out_specs=flat,
        out_shape=jax.ShapeDtypeStruct((LANES, chans), BF16),
        compiler_params=ROOMY,
        name="gate",
    )(toeplitz, entering, query, product, skip, states)


def project_kernel(order, mine, behind, ahead, across_top, across_low, weight, mixed, total):
    step = pl.program_id(0)

    def part(left):
        return jnp.dot(left, weight[...], preferred_element_type=F32)

    @pl.when(step == 0)
    def _():
        total[...] = part(mine[...])

    @pl.when(step == 1)
    def _():
        total[...] += part(behind[...])

    @pl.when(step == 2)
    def _():
        total[...] += part(ahead[...])

    @pl.when(step == 3)
    def _():
        across = jnp.concatenate([across_top[...], across_low[...]], axis=0)
        mixed[...] = (total[...] + part(across)).astype(BF16)


def project(order, pieces, weight):
    tokens, depth = pieces[0].shape
    width = weight.shape[1]
    whole = pl.BlockSpec((tokens, depth), lambda k, order: (0, 0))
    half = pl.BlockSpec((tokens // 2, depth), lambda k, order: (0, 0))
    return pl.pallas_call(
        project_kernel,
        grid_spec=pltpu.PrefetchScalarGridSpec(
            num_scalar_prefetch=1,
            grid=(4,),
            in_specs=[whole, whole, whole, half, half, pl.BlockSpec((depth, width), lambda k, order: (order[k], 0))],
            out_specs=pl.BlockSpec((tokens, width), lambda k, order: (0, 0)),
            scratch_shapes=[pltpu.VMEM((tokens, width), F32)],
        ),
        out_shape=jax.ShapeDtypeStruct((tokens, width), BF16),
        compiler_params=ROOMY,
        name="project",
    )(order, *pieces, weight)


def shifted(x, axis, by):
    count = lax.axis_size(axis)
    return lax.ppermute(x, axis, [(i, (i + by) % count) for i in range(count)])


def on_device(qkv, short_taps, lifetime, residues, skip_gain, segment_starts, out_weight):
    weight = lax.all_gather(out_weight, "seq", axis=0, tiled=True)
    kinds = jnp.transpose(qkv, (1, 0, 2))
    rim = shifted(kinds[:, -(SHORT - 1) :, :], "seq", 1)
    toeplitz, leaving, entering, decay = prepare(segment_starts, lifetime, residues)
    query, product, fresh = features(segment_starts, kinds, rim, short_taps, leaving)
    all_fresh = lax.all_to_all(fresh, "seq", 0, 0, tiled=True)
    all_states = scan_blocks(segment_starts, all_fresh, decay)
    states = lax.all_to_all(all_states, "seq", 0, 0, tiled=True)
    gated = gate(toeplitz, entering, query, product, skip_gain[None, :], states)
    behind = shifted(gated, "fsdp", 1)
    ahead = shifted(gated, "fsdp", -1)
    half = gated.shape[0] // 2
    across_top = shifted(behind[:half], "fsdp", 1)
    across_low = shifted(ahead[half:], "fsdp", -1)
    mine = lax.axis_index("fsdp")
    order = jnp.stack([mine, (mine + 3) % 4, (mine + 1) % 4, (mine + 2) % 4]).astype(jnp.int32)
    return project(order, [gated, behind, ahead, across_top, across_low], weight)


def solution(mesh):
    return jax.shard_map(
        on_device,
        mesh=mesh,
        in_specs=(
            P(("dp", "seq"), None, "fsdp"),
            P(None, None, "fsdp"),
            P("fsdp", None),
            P("fsdp", None),
            P("fsdp"),
            P("dp"),
            P("seq", "fsdp"),
        ),
        out_specs=P(("dp", "seq"), "fsdp"),
        check_vma=False,
    )
```

```python
import jax
import jax.numpy as jnp
from jax import lax
from jax.experimental import pallas as pl
from jax.experimental.pallas import tpu as pltpu
from jax.sharding import PartitionSpec as P

GROUP = 16
MODES = 16
SHORT = 3
LANES = 128
PER_TILE = LANES // GROUP
F32 = jnp.float32
BF16 = jnp.bfloat16
ROOMY = pltpu.CompilerParams(vmem_limit_bytes=20 * 1024 * 1024)
SMEM = pl.BlockSpec(memory_space=pltpu.SMEM)
VMEM = pl.BlockSpec(memory_space=pltpu.VMEM)


def iota(shape, axis):
    return lax.broadcasted_iota(jnp.int32, shape, axis)


def segment_of(starts, positions):
    total = jnp.zeros(positions.shape, jnp.int32)
    for j in range(1, starts.shape[0]):
        total = total + (positions >= starts[j]).astype(jnp.int32)
    return total


def not_start(starts, positions):
    clear = jnp.ones(positions.shape, F32)
    for j in range(starts.shape[0]):
        clear = jnp.where(positions == starts[j], 0.0, clear)
    return clear


def halves(x):
    high = x.astype(BF16)
    return high, (x - high.astype(F32)).astype(BF16)


def doubled(right):
    high, low = halves(right)
    upper = jnp.concatenate([high, low], axis=1)
    lower = jnp.concatenate([high, jnp.zeros_like(low)], axis=1)
    return jnp.concatenate([upper, lower], axis=0)


def split_dot(left, both):
    out = jnp.dot(left, both, preferred_element_type=F32)
    return out[:, :LANES] + out[:, LANES:]


def own_group():
    return (iota((PER_TILE, LANES), 0) == iota((PER_TILE, LANES), 1) // GROUP).astype(F32)


def local_kernel(
    starts, lifetime, residues, qkv, rim, taps, skip, query, base, fresh, entering, decay
):
    tile = pl.program_id(0)
    first = lax.axis_index("seq") * LANES
    rows = iota((LANES, LANES), 0)
    cols = iota((LANES, LANES), 1)
    own = own_group()

    clear = not_start(starts, first + rows)
    clear_before = clear * not_start(starts, first + rows - 1)
    feats = []
    for kind in range(3):
        now = qkv[kind].astype(F32)
        edge = rim[kind].astype(F32)
        one = jnp.where(rows == 0, edge[1:2, :], pltpu.roll(now, 1, 0))
        two = jnp.where(rows == 0, edge[0:1, :], jnp.where(rows == 1, edge[1:2, :], pltpu.roll(now, 2, 0)))
        feats.append(
            taps[0, kind : kind + 1, :] * now
            + taps[1, kind : kind + 1, :] * one * clear
            + taps[2, kind : kind + 1, :] * two * clear_before
        )
    query[...] = feats[0]
    values = feats[1] * feats[2]

    seg_row = segment_of(starts, first + rows)
    seg_col = segment_of(starts, first + cols)
    linked = ((seg_row == seg_col) & (rows >= cols)).astype(F32)
    lane = iota((PER_TILE, LANES), 1)
    seg_lane = segment_of(starts, first + lane)
    last = segment_of(starts, jnp.full((PER_TILE, LANES), first + (LANES - 1)))
    before = jnp.where(first > 0, segment_of(starts, jnp.full((PER_TILE, LANES), first - 1)), -1)
    closing = (seg_lane == last).astype(F32)
    joined = (seg_lane == before).astype(F32)
    offset = lane.astype(F32)
    apart = jnp.where(lane == 0, 0, LANES - lane).astype(F32)

    rate = 1.0 / lifetime[...]
    double = 2.0 * rate
    series = double * (
        1.0
        - double
        * (0.5 - double * (1.0 / 6 - double * (1.0 / 24 - double * (1.0 / 120 - double * (1.0 / 720)))))
    )
    weight = residues[...] * jnp.sqrt(jnp.where(double < 0.07, series, 1.0 - jnp.exp(-double)))
    lags = jnp.zeros((PER_TILE, LANES), F32)
    leave_rows = []
    enter_rows = []
    for mode in range(MODES):
        r = jnp.broadcast_to(rate[:, mode : mode + 1], (PER_TILE, LANES))
        w = jnp.broadcast_to(weight[:, mode : mode + 1], (PER_TILE, LANES))
        lags = lags + w * jnp.exp(-r * apart)
        leave_rows.append(jnp.exp(-r * (LANES - 1.0 - offset)) * closing)
        enter_rows.append(w * jnp.exp(-r * (offset + 1.0)) * joined)
        whole = jnp.sum(jnp.exp(-r * LANES) * own, axis=0, keepdims=True)
        decay[4 * mode + tile // 2, pl.ds(tile % 2, 1), :] = whole
    both = doubled(values)
    high, low = halves(jnp.concatenate(leave_rows, axis=0))
    states = split_dot(jnp.concatenate([high, low], axis=1), both)
    for mode in range(MODES):
        some = states[mode * PER_TILE : (mode + 1) * PER_TILE, :] * own
        fresh[4 * mode + tile // 2, pl.ds(tile % 2, 1), :] = jnp.sum(some, axis=0, keepdims=True)
    high, low = halves(jnp.concatenate(enter_rows, axis=0).T)
    entering[0, :, :LANES] = high
    entering[0, :, LANES:] = low
    total = skip[...] * values
    for group in range(PER_TILE):
        spread = jnp.broadcast_to(lags[group : group + 1, :], (LANES, LANES))
        rolled = pltpu.roll(spread, 0, 1, stride=1, stride_axis=0)
        high, low = halves(rolled * linked)
        out = split_dot(jnp.concatenate([high, low], axis=1), both)
        total = total + jnp.where(cols // GROUP == group, out, 0.0)
    base[...] = total


def local_work(starts, lifetime, residues, qkv, rim, taps, skip):
    chans = qkv.shape[2]
    tiles = chans // LANES
    flat = pl.BlockSpec((LANES, LANES), lambda k: (0, k))
    small = pl.BlockSpec((PER_TILE, MODES), lambda k: (k, 0))
    whole = pl.BlockSpec((8 * tiles, 2, LANES), lambda k: (0, 0, 0))
    return pl.pallas_call(
        local_kernel,
        grid=(tiles,),
        in_specs=[
            SMEM,
            small,
            small,
            pl.BlockSpec((3, LANES, LANES), lambda k: (0, 0, k)),
            pl.BlockSpec((3, SHORT - 1, LANES), lambda k: (0, 0, k)),
            pl.BlockSpec((SHORT, 3, LANES), lambda k: (0, 0, k)),
            pl.BlockSpec((1, LANES), lambda k: (0, k)),
        ],
        out_specs=[flat, flat, whole, pl.BlockSpec((1, LANES, 2 * LANES), lambda k: (k, 0, 0)), whole],
        out_shape=[
            jax.ShapeDtypeStruct((LANES, chans), F32),
            jax.ShapeDtypeStruct((LANES, chans), F32),
            jax.ShapeDtypeStruct((8 * tiles, 2, LANES), F32),
            jax.ShapeDtypeStruct((tiles, LANES, 2 * LANES), BF16),
            jax.ShapeDtypeStruct((8 * tiles, 2, LANES), F32),
        ],
        compiler_params=ROOMY,
        name="local_work",
    )(starts, lifetime, residues, qkv, rim, taps, skip)


def scan_kernel(starts, fresh, decay, entering):
    blocks = fresh.shape[0]
    whole = decay[lax.axis_index("seq")]
    gate = jnp.ones((blocks, 2, LANES), F32)
    number = iota((blocks, 2, LANES), 0)
    for j in range(1, starts.shape[0]):
        gate = jnp.where(number == starts[j] // LANES, 0.0, gate)
    state = jnp.zeros((2, LANES), F32)
    for block in range(blocks):
        entering[block] = state
        state = state * (whole * gate[block]) + fresh[block]


def scan_blocks(starts, fresh, decay):
    return pl.pallas_call(
        scan_kernel,
        in_specs=[SMEM, VMEM, VMEM],
        out_specs=VMEM,
        out_shape=jax.ShapeDtypeStruct(fresh.shape, F32),
        name="scan_blocks",
    )(starts, fresh, decay)


def gate_kernel(entering, query, base, states, gated):
    tile = pl.program_id(0)
    own = own_group()
    spread = []
    for mode in range(MODES):
        state = states[4 * mode + tile // 2, pl.ds(tile % 2, 1), :]
        spread.append(jnp.broadcast_to(state, (PER_TILE, LANES)) * own)
    carried = split_dot(entering[0], doubled(jnp.concatenate(spread, axis=0)))
    gated[...] = (query[...] * (base[...] + carried)).astype(BF16)


def gate(entering, query, base, states):
    chans = query.shape[1]
    flat = pl.BlockSpec((LANES, LANES), lambda k: (0, k))
    return pl.pallas_call(
        gate_kernel,
        grid=(chans // LANES,),
        in_specs=[pl.BlockSpec((1, LANES, 2 * LANES), lambda k: (k, 0, 0)), flat, flat, VMEM],
        out_specs=flat,
        out_shape=jax.ShapeDtypeStruct((LANES, chans), BF16),
        compiler_params=ROOMY,
        name="gate",
    )(entering, query, base, states)


def project_kernel(order, mine, behind, ahead, across_top, across_low, weight, mixed, total):
    step = pl.program_id(0)

    def part(left):
        block = weight[...].reshape(left.shape[1], weight.shape[3])
        return jnp.dot(left, block, preferred_element_type=F32)

    @pl.when(step == 0)
    def _():
        total[...] = part(mine[...])

    @pl.when(step == 1)
    def _():
        total[...] += part(behind[...])

    @pl.when(step == 2)
    def _():
        total[...] += part(ahead[...])

    @pl.when(step == 3)
    def _():
        across = jnp.concatenate([across_top[...], across_low[...]], axis=0)
        mixed[...] = (total[...] + part(across)).astype(BF16)


def project(order, pieces, weight):
    tokens, depth = pieces[0].shape
    outer, planes, rows, width = weight.shape
    whole = pl.BlockSpec((tokens, depth), lambda k, order: (0, 0))
    half = pl.BlockSpec((tokens // 2, depth), lambda k, order: (0, 0))
    block = pl.BlockSpec((outer, 1, rows, width), lambda k, order: (0, order[k], 0, 0))
    return pl.pallas_call(
        project_kernel,
        grid_spec=pltpu.PrefetchScalarGridSpec(
            num_scalar_prefetch=1,
            grid=(planes,),
            in_specs=[whole, whole, whole, half, half, block],
            out_specs=pl.BlockSpec((tokens, width), lambda k, order: (0, 0)),
            scratch_shapes=[pltpu.VMEM((tokens, width), F32)],
        ),
        out_shape=jax.ShapeDtypeStruct((tokens, width), BF16),
        compiler_params=ROOMY,
        name="project",
    )(order, *pieces, weight)


def shifted(x, axis, by):
    count = lax.axis_size(axis)
    return lax.ppermute(x, axis, [(i, (i + by) % count) for i in range(count)])


PLANES = 4


def gather_weight(out_weight):
    count = lax.axis_size("seq")
    inner = count // PLANES
    rows, width = out_weight.shape
    parts = [out_weight] + [shifted(out_weight, "seq", inner * j) for j in range(1, PLANES)]
    column = jnp.concatenate(parts, axis=0)
    groups = [list(range(x * inner, (x + 1) * inner)) for x in range(PLANES)]
    whole = lax.all_gather(column, "seq", axis=0, tiled=True, axis_index_groups=groups)
    return whole.reshape(inner, PLANES, rows, width)


def on_device(qkv, short_taps, lifetime, residues, skip_gain, segment_starts, out_weight):
    kinds = jnp.transpose(qkv, (1, 0, 2))
    rim = shifted(kinds[:, -(SHORT - 1) :, :], "seq", 1)
    weight = gather_weight(out_weight)
    query, base, fresh, entering, decay = local_work(
        segment_starts, lifetime, residues, kinds, rim, short_taps, skip_gain[None, :]
    )
    all_fresh = lax.all_to_all(fresh, "seq", 0, 0, tiled=True)
    all_states = scan_blocks(segment_starts, all_fresh, decay)
    states = lax.all_to_all(all_states, "seq", 0, 0, tiled=True)
    gated = gate(entering, query, base, states)
    behind = shifted(gated, "fsdp", 1)
    ahead = shifted(gated, "fsdp", -1)
    half = gated.shape[0] // 2
    across_top = shifted(behind[:half], "fsdp", 1)
    across_low = shifted(ahead[half:], "fsdp", -1)
    mine = lax.axis_index("fsdp")
    plane = lax.axis_index("seq") // (lax.axis_size("seq") // PLANES)
    held = jnp.stack([mine, mine - 1, mine + 1, mine + 2])
    order = ((plane - held + 2 * PLANES) % PLANES).astype(jnp.int32)
    return project(order, [gated, behind, ahead, across_top, across_low], weight)


def solution(mesh):
    return jax.shard_map(
        on_device,
        mesh=mesh,
        in_specs=(
            P(("dp", "seq"), None, "fsdp"),
            P(None, None, "fsdp"),
            P("fsdp", None),
            P("fsdp", None),
            P("fsdp"),
            P("dp"),
            P("seq", "fsdp"),
        ),
        out_specs=P(("dp", "seq"), "fsdp"),
        check_vma=False,
    )
```

```python
import jax
import jax.numpy as jnp
from jax import lax
from jax.experimental import pallas as pl
from jax.experimental.pallas import tpu as pltpu
from jax.sharding import PartitionSpec as P

GROUP = 16
MODES = 16
SHORT = 3
LANES = 128
PER_TILE = LANES // GROUP
F32 = jnp.float32
BF16 = jnp.bfloat16
ROOMY = pltpu.CompilerParams(vmem_limit_bytes=60 * 1024 * 1024)
SMEM = pl.BlockSpec(memory_space=pltpu.SMEM)
VMEM = pl.BlockSpec(memory_space=pltpu.VMEM)


def iota(shape, axis):
    return lax.broadcasted_iota(jnp.int32, shape, axis)


def segment_of(starts, positions):
    total = jnp.zeros(positions.shape, jnp.int32)
    for j in range(1, starts.shape[0]):
        total = total + (positions >= starts[j]).astype(jnp.int32)
    return total


def not_start(starts, positions):
    clear = jnp.ones(positions.shape, F32)
    for j in range(starts.shape[0]):
        clear = jnp.where(positions == starts[j], 0.0, clear)
    return clear


def halves(x):
    high = x.astype(BF16)
    return high, (x - high.astype(F32)).astype(BF16)


def doubled(right):
    high, low = halves(right)
    upper = jnp.concatenate([high, low], axis=1)
    lower = jnp.concatenate([high, jnp.zeros_like(low)], axis=1)
    return jnp.concatenate([upper, lower], axis=0)


def split_dot(left, both):
    out = jnp.dot(left, both, preferred_element_type=F32)
    return out[:, :LANES] + out[:, LANES:]


def own_group():
    return (iota((PER_TILE, LANES), 0) == iota((PER_TILE, LANES), 1) // GROUP).astype(F32)


def local_kernel(
    starts, lifetime, residues, qkv, rim, taps, skip, query, base, fresh, entering, decay
):
    tile = pl.program_id(0)
    first = lax.axis_index("seq") * LANES
    rows = iota((LANES, LANES), 0)
    cols = iota((LANES, LANES), 1)
    own = own_group()

    clear = not_start(starts, first + rows)
    clear_before = clear * not_start(starts, first + rows - 1)
    feats = []
    for kind in range(3):
        now = qkv[kind].astype(F32)
        edge = rim[kind].astype(F32)
        one = jnp.where(rows == 0, edge[1:2, :], pltpu.roll(now, 1, 0))
        two = jnp.where(rows == 0, edge[0:1, :], jnp.where(rows == 1, edge[1:2, :], pltpu.roll(now, 2, 0)))
        feats.append(
            taps[0, kind : kind + 1, :] * now
            + taps[1, kind : kind + 1, :] * one * clear
            + taps[2, kind : kind + 1, :] * two * clear_before
        )
    query[...] = feats[0]
    values = feats[1] * feats[2]

    seg_row = segment_of(starts, first + rows)
    seg_col = segment_of(starts, first + cols)
    linked = ((seg_row == seg_col) & (rows >= cols)).astype(F32)
    lane = iota((PER_TILE, LANES), 1)
    seg_lane = segment_of(starts, first + lane)
    last = segment_of(starts, jnp.full((PER_TILE, LANES), first + (LANES - 1)))
    before = jnp.where(first > 0, segment_of(starts, jnp.full((PER_TILE, LANES), first - 1)), -1)
    closing = (seg_lane == last).astype(F32)
    joined = (seg_lane == before).astype(F32)
    offset = lane.astype(F32)
    apart = jnp.where(lane == 0, 0, LANES - lane).astype(F32)

    rate = 1.0 / lifetime[...]
    double = 2.0 * rate
    series = double * (
        1.0
        - double
        * (0.5 - double * (1.0 / 6 - double * (1.0 / 24 - double * (1.0 / 120 - double * (1.0 / 720)))))
    )
    weight = residues[...] * jnp.sqrt(jnp.where(double < 0.07, series, 1.0 - jnp.exp(-double)))
    lags = jnp.zeros((PER_TILE, LANES), F32)
    leave_rows = []
    enter_rows = []
    for mode in range(MODES):
        r = jnp.broadcast_to(rate[:, mode : mode + 1], (PER_TILE, LANES))
        w = jnp.broadcast_to(weight[:, mode : mode + 1], (PER_TILE, LANES))
        lags = lags + w * jnp.exp(-r * apart)
        leave_rows.append(jnp.exp(-r * (LANES - 1.0 - offset)) * closing)
        enter_rows.append(w * jnp.exp(-r * (offset + 1.0)) * joined)
        whole = jnp.sum(jnp.exp(-r * LANES) * own, axis=0, keepdims=True)
        decay[4 * mode + tile // 2, pl.ds(tile % 2, 1), :] = whole
    both = doubled(values)
    high, low = halves(jnp.concatenate(leave_rows, axis=0))
    states = split_dot(jnp.concatenate([high, low], axis=1), both)
    for mode in range(MODES):
        some = states[mode * PER_TILE : (mode + 1) * PER_TILE, :] * own
        fresh[4 * mode + tile // 2, pl.ds(tile % 2, 1), :] = jnp.sum(some, axis=0, keepdims=True)
    high, low = halves(jnp.concatenate(enter_rows, axis=0).T)
    entering[0, :, :LANES] = high
    entering[0, :, LANES:] = low
    total = skip[...] * values
    for group in range(PER_TILE):
        spread = jnp.broadcast_to(lags[group : group + 1, :], (LANES, LANES))
        rolled = pltpu.roll(spread, 0, 1, stride=1, stride_axis=0)
        high, low = halves(rolled * linked)
        out = split_dot(jnp.concatenate([high, low], axis=1), both)
        total = total + jnp.where(cols // GROUP == group, out, 0.0)
    base[...] = total


def local_work(starts, lifetime, residues, qkv, rim, taps, skip):
    chans = qkv.shape[2]
    tiles = chans // LANES
    flat = pl.BlockSpec((LANES, LANES), lambda k: (0, k))
    small = pl.BlockSpec((PER_TILE, MODES), lambda k: (k, 0))
    whole = pl.BlockSpec((8 * tiles, 2, LANES), lambda k: (0, 0, 0))
    return pl.pallas_call(
        local_kernel,
        grid=(tiles,),
        in_specs=[
            SMEM,
            small,
            small,
            pl.BlockSpec((3, LANES, LANES), lambda k: (0, 0, k)),
            pl.BlockSpec((3, SHORT - 1, LANES), lambda k: (0, 0, k)),
            pl.BlockSpec((SHORT, 3, LANES), lambda k: (0, 0, k)),
            pl.BlockSpec((1, LANES), lambda k: (0, k)),
        ],
        out_specs=[flat, flat, whole, pl.BlockSpec((1, LANES, 2 * LANES), lambda k: (k, 0, 0)), whole],
        out_shape=[
            jax.ShapeDtypeStruct((LANES, chans), F32),
            jax.ShapeDtypeStruct((LANES, chans), F32),
            jax.ShapeDtypeStruct((8 * tiles, 2, LANES), F32),
            jax.ShapeDtypeStruct((tiles, LANES, 2 * LANES), BF16),
            jax.ShapeDtypeStruct((8 * tiles, 2, LANES), F32),
        ],
        compiler_params=ROOMY,
        name="local_work",
    )(starts, lifetime, residues, qkv, rim, taps, skip)


def scan_kernel(starts, fresh, decay, entering):
    blocks = fresh.shape[0]
    whole = decay[lax.axis_index("seq")]
    gate = jnp.ones((blocks, 2, LANES), F32)
    number = iota((blocks, 2, LANES), 0)
    for j in range(1, starts.shape[0]):
        gate = jnp.where(number == starts[j] // LANES, 0.0, gate)
    state = jnp.zeros((2, LANES), F32)
    for block in range(blocks):
        entering[block] = state
        state = state * (whole * gate[block]) + fresh[block]


def scan_blocks(starts, fresh, decay):
    return pl.pallas_call(
        scan_kernel,
        in_specs=[SMEM, VMEM, VMEM],
        out_specs=VMEM,
        out_shape=jax.ShapeDtypeStruct(fresh.shape, F32),
        name="scan_blocks",
    )(starts, fresh, decay)


def gate_kernel(entering, query, base, states, copies):
    tile = pl.program_id(0)
    own = own_group()
    spread = []
    for mode in range(MODES):
        state = states[4 * mode + tile // 2, pl.ds(tile % 2, 1), :]
        spread.append(jnp.broadcast_to(state, (PER_TILE, LANES)) * own)
    carried = split_dot(entering[0], doubled(jnp.concatenate(spread, axis=0)))
    gated = (query[...] * (base[...] + carried)).astype(BF16)
    for copy in range(copies.shape[0]):
        copies[copy] = gated


def gate(entering, query, base, states, count):
    chans = query.shape[1]
    flat = pl.BlockSpec((LANES, LANES), lambda k: (0, k))
    return pl.pallas_call(
        gate_kernel,
        grid=(chans // LANES,),
        in_specs=[pl.BlockSpec((1, LANES, 2 * LANES), lambda k: (k, 0, 0)), flat, flat, VMEM],
        out_specs=pl.BlockSpec((count, LANES, LANES), lambda k: (0, 0, k)),
        out_shape=jax.ShapeDtypeStruct((count, LANES, chans), BF16),
        compiler_params=ROOMY,
        name="gate",
    )(entering, query, base, states)


def project_kernel(gated, weight, mixed, total):
    step = pl.program_id(0)
    block = weight[...].reshape(gated.shape[2], weight.shape[3])
    part = jnp.dot(gated[0], block, preferred_element_type=F32)

    @pl.when(step == 0)
    def _():
        total[...] = part

    @pl.when(step > 0)
    def _():
        total[...] += part

    @pl.when(step == pl.num_programs(0) - 1)
    def _():
        mixed[...] = total[...].astype(BF16)


def project(gated, weight):
    planes, tokens, depth = gated.shape
    outer, _, rows, width = weight.shape
    return pl.pallas_call(
        project_kernel,
        grid=(planes,),
        in_specs=[
            pl.BlockSpec((1, tokens, depth), lambda k: (k, 0, 0)),
            pl.BlockSpec((outer, 1, rows, width), lambda k: (0, k, 0, 0)),
        ],
        out_specs=pl.BlockSpec((tokens, width), lambda k: (0, 0)),
        out_shape=jax.ShapeDtypeStruct((tokens, width), BF16),
        scratch_shapes=[pltpu.VMEM((tokens, width), F32)],
        compiler_params=ROOMY,
        name="project",
    )(gated, weight)


def shifted(x, axis, by):
    count = lax.axis_size(axis)
    return lax.ppermute(x, axis, [(i, (i + by) % count) for i in range(count)])


PLANES = 4


def gather_weight(out_weight):
    count = lax.axis_size("seq")
    inner = count // PLANES
    rows, width = out_weight.shape
    lines = [list(range(j, count, inner)) for j in range(inner)]
    copies = jnp.broadcast_to(out_weight[None], (PLANES, rows, width))
    column = lax.all_to_all(copies, "seq", 0, 0, tiled=True, axis_index_groups=lines)
    planes = [list(range(x * inner, (x + 1) * inner)) for x in range(PLANES)]
    return lax.all_gather(column, "seq", axis=0, tiled=False, axis_index_groups=planes)


def on_device(qkv, short_taps, lifetime, residues, skip_gain, segment_starts, out_weight):
    kinds = jnp.transpose(qkv, (1, 0, 2))
    rim = shifted(kinds[:, -(SHORT - 1) :, :], "seq", 1)
    weight = gather_weight(out_weight)
    query, base, fresh, entering, decay = local_work(
        segment_starts, lifetime, residues, kinds, rim, short_taps, skip_gain[None, :]
    )
    all_fresh = lax.all_to_all(fresh, "seq", 0, 0, tiled=True)
    all_states = scan_blocks(segment_starts, all_fresh, decay)
    states = lax.all_to_all(all_states, "seq", 0, 0, tiled=True)
    copies = gate(entering, query, base, states, PLANES)
    gated = lax.all_to_all(copies, "fsdp", 0, 0, tiled=True)
    return project(gated, weight)


def solution(mesh):
    return jax.shard_map(
        on_device,
        mesh=mesh,
        in_specs=(
            P(("dp", "seq"), None, "fsdp"),
            P(None, None, "fsdp"),
            P("fsdp", None),
            P("fsdp", None),
            P("fsdp"),
            P("dp"),
            P("seq", "fsdp"),
        ),
        out_specs=P(("dp", "seq"), "fsdp"),
        check_vma=False,
    )
```

```python
import jax
import jax.numpy as jnp
from jax import lax
from jax.experimental import pallas as pl
from jax.experimental.pallas import tpu as pltpu
from jax.sharding import PartitionSpec as P

GROUP = 16
MODES = 16
SHORT = 3
LANES = 128
PER_TILE = LANES // GROUP
F32 = jnp.float32
BF16 = jnp.bfloat16
ROOMY = pltpu.CompilerParams(vmem_limit_bytes=60 * 1024 * 1024)
SMEM = pl.BlockSpec(memory_space=pltpu.SMEM)
VMEM = pl.BlockSpec(memory_space=pltpu.VMEM)


def iota(shape, axis):
    return lax.broadcasted_iota(jnp.int32, shape, axis)


def segment_of(starts, positions):
    total = jnp.zeros(positions.shape, jnp.int32)
    for j in range(1, starts.shape[0]):
        total = total + (positions >= starts[j]).astype(jnp.int32)
    return total


def not_start(starts, positions):
    clear = jnp.ones(positions.shape, F32)
    for j in range(starts.shape[0]):
        clear = jnp.where(positions == starts[j], 0.0, clear)
    return clear


def halves(x):
    high = x.astype(BF16)
    return high, (x - high.astype(F32)).astype(BF16)


def doubled(right):
    high, low = halves(right)
    upper = jnp.concatenate([high, low], axis=1)
    lower = jnp.concatenate([high, jnp.zeros_like(low)], axis=1)
    return jnp.concatenate([upper, lower], axis=0)


def split_dot(left, both):
    out = jnp.dot(left, both, preferred_element_type=F32)
    return out[:, :LANES] + out[:, LANES:]


def own_group():
    return (iota((PER_TILE, LANES), 0) == iota((PER_TILE, LANES), 1) // GROUP).astype(F32)


def turned(x):
    wide = jnp.concatenate([x, jnp.zeros((x.shape[0], LANES - x.shape[1]), F32)], axis=1)
    return jnp.concatenate([wide, jnp.zeros((LANES - x.shape[0], LANES), F32)], axis=0).T


LOCAL_TILES = 2


def local_kernel(
    starts, lifetime, residues, qkv, rim, taps, skip, query, base, fresh, entering, decay, rates, weights
):
    step = pl.program_id(0)
    first = lax.axis_index("seq") * LANES
    rows = iota((LANES, LANES), 0)
    cols = iota((LANES, LANES), 1)
    own = own_group()

    @pl.when(step == 0)
    def _():
        rate = 1.0 / lifetime[...]
        double = 2.0 * rate
        series = double * (
            1.0
            - double
            * (0.5 - double * (1.0 / 6 - double * (1.0 / 24 - double * (1.0 / 120 - double * (1.0 / 720)))))
        )
        rates[...] = turned(rate)
        weights[...] = turned(residues[...] * jnp.sqrt(jnp.where(double < 0.07, series, 1.0 - jnp.exp(-double))))

    clear = not_start(starts, first + rows)
    clear_before = clear * not_start(starts, first + rows - 1)
    seg_row = segment_of(starts, first + rows)
    seg_col = segment_of(starts, first + cols)
    linked = ((seg_row == seg_col) & (rows >= cols)).astype(F32)
    lane = iota((PER_TILE, LANES), 1)
    seg_lane = seg_col[:PER_TILE]
    last = segment_of(starts, jnp.full((PER_TILE, LANES), first + (LANES - 1)))
    before = jnp.where(first > 0, segment_of(starts, jnp.full((PER_TILE, LANES), first - 1)), -1)
    closing = (seg_lane == last).astype(F32)
    joined = (seg_lane == before).astype(F32)
    offset = lane.astype(F32)
    apart = jnp.where(lane == 0, 0, LANES - lane).astype(F32)

    for part in range(LOCAL_TILES):
        tile = step * LOCAL_TILES + part
        span = slice(part * LANES, (part + 1) * LANES)
        feats = []
        for kind in range(3):
            now = qkv[kind, :, span].astype(F32)
            edge = rim[kind, :, span].astype(F32)
            one = jnp.where(rows == 0, edge[1:2, :], pltpu.roll(now, 1, 0))
            two = jnp.where(rows == 0, edge[0:1, :], jnp.where(rows == 1, edge[1:2, :], pltpu.roll(now, 2, 0)))
            feats.append(
                taps[0, kind : kind + 1, span] * now
                + taps[1, kind : kind + 1, span] * one * clear
                + taps[2, kind : kind + 1, span] * two * clear_before
            )
        query[:, span] = feats[0]
        values = feats[1] * feats[2]

        group_rows = pl.ds(pl.multiple_of(tile * PER_TILE, PER_TILE), PER_TILE)
        rate = rates[group_rows, :]
        weight = weights[group_rows, :]
        lags = jnp.zeros((PER_TILE, LANES), F32)
        leave_rows = []
        enter_rows = []
        for mode in range(MODES):
            r = jnp.broadcast_to(rate[:, mode : mode + 1], (PER_TILE, LANES))
            w = jnp.broadcast_to(weight[:, mode : mode + 1], (PER_TILE, LANES))
            lags = lags + w * jnp.exp(-r * apart)
            leave_rows.append(jnp.exp(-r * (LANES - 1.0 - offset)) * closing)
            enter_rows.append(w * jnp.exp(-r * (offset + 1.0)) * joined)
            whole = jnp.sum(jnp.exp(-r * LANES) * own, axis=0, keepdims=True)
            decay[4 * mode + tile // 2, pl.ds(tile % 2, 1), :] = whole
        both = doubled(values)
        high, low = halves(jnp.concatenate(leave_rows, axis=0))
        states = split_dot(jnp.concatenate([high, low], axis=1), both)
        for mode in range(MODES):
            some = states[mode * PER_TILE : (mode + 1) * PER_TILE, :] * own
            fresh[4 * mode + tile // 2, pl.ds(tile % 2, 1), :] = jnp.sum(some, axis=0, keepdims=True)
        high, low = halves(jnp.concatenate(enter_rows, axis=0).T)
        entering[part, :, :LANES] = high
        entering[part, :, LANES:] = low
        total = skip[:, span] * values
        for group in range(PER_TILE):
            spread = jnp.broadcast_to(lags[group : group + 1, :], (LANES, LANES))
            rolled = pltpu.roll(spread, 0, 1, stride=1, stride_axis=0)
            high, low = halves(rolled * linked)
            out = split_dot(jnp.concatenate([high, low], axis=1), both)
            total = total + jnp.where(cols // GROUP == group, out, 0.0)
        base[:, span] = total


def local_work(starts, lifetime, residues, qkv, rim, taps, skip):
    chans = qkv.shape[2]
    tiles = chans // LANES
    width = LOCAL_TILES * LANES
    flat = pl.BlockSpec((LANES, width), lambda k: (0, k))
    small = pl.BlockSpec(lifetime.shape, lambda k: (0, 0))
    whole = pl.BlockSpec((8 * tiles, 2, LANES), lambda k: (0, 0, 0))
    return pl.pallas_call(
        local_kernel,
        grid=(tiles // LOCAL_TILES,),
        in_specs=[
            SMEM,
            small,
            small,
            pl.BlockSpec((3, LANES, width), lambda k: (0, 0, k)),
            pl.BlockSpec((3, SHORT - 1, width), lambda k: (0, 0, k)),
            pl.BlockSpec((SHORT, 3, width), lambda k: (0, 0, k)),
            pl.BlockSpec((1, width), lambda k: (0, k)),
        ],
        out_specs=[
            flat,
            flat,
            whole,
            pl.BlockSpec((LOCAL_TILES, LANES, 2 * LANES), lambda k: (k, 0, 0)),
            whole,
        ],
        out_shape=[
            jax.ShapeDtypeStruct((LANES, chans), F32),
            jax.ShapeDtypeStruct((LANES, chans), F32),
            jax.ShapeDtypeStruct((8 * tiles, 2, LANES), F32),
            jax.ShapeDtypeStruct((tiles, LANES, 2 * LANES), BF16),
            jax.ShapeDtypeStruct((8 * tiles, 2, LANES), F32),
        ],
        scratch_shapes=[pltpu.VMEM((LANES, LANES), F32), pltpu.VMEM((LANES, LANES), F32)],
        compiler_params=ROOMY,
        name="local_work",
    )(starts, lifetime, residues, qkv, rim, taps, skip)


def scan_kernel(starts, fresh, decay, entering):
    blocks = fresh.shape[0]
    whole = decay[lax.axis_index("seq")]
    gate = jnp.ones((blocks, 2, LANES), F32)
    number = iota((blocks, 2, LANES), 0)
    for j in range(1, starts.shape[0]):
        gate = jnp.where(number == starts[j] // LANES, 0.0, gate)
    state = jnp.zeros((2, LANES), F32)
    for block in range(blocks):
        entering[block] = state
        state = state * (whole * gate[block]) + fresh[block]


def scan_blocks(starts, fresh, decay):
    return pl.pallas_call(
        scan_kernel,
        in_specs=[SMEM, VMEM, VMEM],
        out_specs=VMEM,
        out_shape=jax.ShapeDtypeStruct(fresh.shape, F32),
        name="scan_blocks",
    )(starts, fresh, decay)


GATE_TILES = 4


def gate_kernel(entering, query, base, states, copies):
    own = own_group()
    for part in range(GATE_TILES):
        tile = pl.program_id(0) * GATE_TILES + part
        span = slice(part * LANES, (part + 1) * LANES)
        spread = []
        for mode in range(MODES):
            state = states[4 * mode + tile // 2, pl.ds(tile % 2, 1), :]
            spread.append(jnp.broadcast_to(state, (PER_TILE, LANES)) * own)
        carried = split_dot(entering[part], doubled(jnp.concatenate(spread, axis=0)))
        gated = (query[:, span] * (base[:, span] + carried)).astype(BF16)
        for copy in range(copies.shape[0]):
            copies[copy, :, span] = gated


def gate(entering, query, base, states, count):
    chans = query.shape[1]
    width = GATE_TILES * LANES
    flat = pl.BlockSpec((LANES, width), lambda k: (0, k))
    return pl.pallas_call(
        gate_kernel,
        grid=(chans // width,),
        in_specs=[pl.BlockSpec((GATE_TILES, LANES, 2 * LANES), lambda k: (k, 0, 0)), flat, flat, VMEM],
        out_specs=pl.BlockSpec((count, LANES, width), lambda k: (0, 0, k)),
        out_shape=jax.ShapeDtypeStruct((count, LANES, chans), BF16),
        compiler_params=ROOMY,
        name="gate",
    )(entering, query, base, states)


def project_kernel(gated, weight, mixed, held, sems):
    planes = gated.shape[0]
    outer = weight.shape[0]
    half = outer // 2
    here = lax.axis_index("seq") // outer

    def copy(plane, part):
        some = pl.ds(part * half, half)
        return pltpu.make_async_copy(weight.at[some, plane], held.at[plane, some], sems.at[plane, part])

    for plane in range(planes):
        for part in range(2):
            copy(plane, part).start()
    depth = gated.shape[2] // 2
    total = jnp.zeros(mixed.shape, F32)
    for plane in range(planes):
        for part in range(2):
            copy(plane, part).wait()
            block = held[plane, part * half : (part + 1) * half].reshape(depth, mixed.shape[1])
            left = gated[lax.rem(here - plane + planes, planes), :, part * depth : (part + 1) * depth]
            total = total + jnp.dot(left, block, preferred_element_type=F32)
    mixed[...] = total.astype(BF16)


def project(gated, weight):
    planes, tokens, _ = gated.shape
    outer, _, rows, width = weight.shape
    return pl.pallas_call(
        project_kernel,
        in_specs=[VMEM, pl.BlockSpec(memory_space=pl.ANY)],
        out_specs=VMEM,
        out_shape=jax.ShapeDtypeStruct((tokens, width), BF16),
        scratch_shapes=[
            pltpu.VMEM((planes, outer, rows, width), BF16),
            pltpu.SemaphoreType.DMA((planes, 2)),
        ],
        compiler_params=ROOMY,
        name="project",
    )(gated, weight)


def shifted(x, axis, by):
    count = lax.axis_size(axis)
    return lax.ppermute(x, axis, [(i, (i + by) % count) for i in range(count)])


PLANES = 4


def on_device(qkv, short_taps, lifetime, residues, skip_gain, segment_starts, out_weight):
    kinds = jnp.transpose(qkv, (1, 0, 2))
    inner = lax.axis_size("seq") // PLANES
    edge, own_rows = lax.optimization_barrier((kinds[:, -(SHORT - 1) :, :], out_weight))
    arrived = [shifted(edge, "seq", 1)] + [shifted(own_rows, "seq", inner * j) for j in range(1, PLANES)]
    rim, *others = lax.optimization_barrier(arrived)
    column = jnp.concatenate([own_rows] + others, axis=0).reshape(PLANES, *out_weight.shape)
    groups = [list(range(x * inner, (x + 1) * inner)) for x in range(PLANES)]
    weight = lax.all_gather(column, "seq", axis=0, tiled=False, axis_index_groups=groups)

    query, base, fresh, entering, decay = local_work(
        segment_starts, lifetime.T, residues.T, kinds, rim, short_taps, skip_gain[None, :]
    )
    all_fresh = lax.all_to_all(fresh, "seq", 0, 0, tiled=True)
    all_states = scan_blocks(segment_starts, all_fresh, decay)
    states = lax.all_to_all(all_states, "seq", 0, 0, tiled=True)
    copies = gate(entering, query, base, states, PLANES)
    gated = lax.all_to_all(copies, "fsdp", 0, 0, tiled=True)
    return project(gated, weight)


def solution(mesh):
    return jax.shard_map(
        on_device,
        mesh=mesh,
        in_specs=(
            P(("dp", "seq"), None, "fsdp"),
            P(None, None, "fsdp"),
            P("fsdp", None),
            P("fsdp", None),
            P("fsdp"),
            P("dp"),
            P("seq", "fsdp"),
        ),
        out_specs=P(("dp", "seq"), "fsdp"),
        check_vma=False,
    )
```

```python
import functools

import jax
import jax.numpy as jnp
from jax import lax
from jax.experimental import pallas as pl
from jax.experimental.pallas import tpu as pltpu
from jax.sharding import PartitionSpec as P

GROUP = 16
MODES = 16
SHORT = 3
LANES = 128
PER_TILE = LANES // GROUP
F32 = jnp.float32
BF16 = jnp.bfloat16
ROOMY = pltpu.CompilerParams(vmem_limit_bytes=60 * 1024 * 1024)
MODEST = pltpu.CompilerParams(vmem_limit_bytes=24 * 1024 * 1024)
SMEM = pl.BlockSpec(memory_space=pltpu.SMEM)
VMEM = pl.BlockSpec(memory_space=pltpu.VMEM)


def iota(shape, axis):
    return lax.broadcasted_iota(jnp.int32, shape, axis)


def segment_of(starts, positions):
    total = jnp.zeros(positions.shape, jnp.int32)
    for j in range(1, starts.shape[0]):
        total = total + (positions >= starts[j]).astype(jnp.int32)
    return total


def not_start(starts, positions):
    clear = jnp.ones(positions.shape, F32)
    for j in range(starts.shape[0]):
        clear = jnp.where(positions == starts[j], 0.0, clear)
    return clear


def halves(x):
    high = x.astype(BF16)
    return high, (x - high.astype(F32)).astype(BF16)


def doubled(right):
    high, low = halves(right)
    upper = jnp.concatenate([high, low], axis=1)
    lower = jnp.concatenate([high, jnp.zeros_like(low)], axis=1)
    return jnp.concatenate([upper, lower], axis=0)


def split_dot(left, both):
    out = jnp.dot(left, both, preferred_element_type=F32)
    return out[:, :LANES] + out[:, LANES:]


def own_group():
    return (iota((PER_TILE, LANES), 0) == iota((PER_TILE, LANES), 1) // GROUP).astype(F32)


def turned(x):
    wide = jnp.concatenate([x, jnp.zeros((x.shape[0], LANES - x.shape[1]), F32)], axis=1)
    return jnp.concatenate([wide, jnp.zeros((LANES - x.shape[0], LANES), F32)], axis=0).T


FEATURE_TILES = 2


def features_kernel(
    starts, lifetime, residues, qkv, rim, taps, query, product, fresh, lags, entering, decay, rates, weights
):
    step = pl.program_id(0)
    first = lax.axis_index("seq") * LANES
    rows = iota((LANES, LANES), 0)
    own = own_group()

    @pl.when(step == 0)
    def _():
        rate = 1.0 / lifetime[...]
        double = 2.0 * rate
        series = double * (
            1.0
            - double
            * (0.5 - double * (1.0 / 6 - double * (1.0 / 24 - double * (1.0 / 120 - double * (1.0 / 720)))))
        )
        rates[...] = turned(rate)
        weights[...] = turned(residues[...] * jnp.sqrt(jnp.where(double < 0.07, series, 1.0 - jnp.exp(-double))))

    clear = not_start(starts, first + rows)
    clear_before = clear * not_start(starts, first + rows - 1)
    lane = iota((PER_TILE, LANES), 1)
    seg_lane = segment_of(starts, first + lane)
    last = segment_of(starts, jnp.full((PER_TILE, LANES), first + (LANES - 1)))
    before = jnp.where(first > 0, segment_of(starts, jnp.full((PER_TILE, LANES), first - 1)), -1)
    closing = (seg_lane == last).astype(F32)
    joined = (seg_lane == before).astype(F32)
    offset = lane.astype(F32)
    apart = jnp.where(lane == 0, 0, LANES - lane).astype(F32)

    for part in range(FEATURE_TILES):
        tile = step * FEATURE_TILES + part
        span = slice(part * LANES, (part + 1) * LANES)
        feats = []
        for kind in range(3):
            now = qkv[kind, :, span].astype(F32)
            edge = rim[kind, :, span].astype(F32)
            one = jnp.where(rows == 0, edge[1:2, :], pltpu.roll(now, 1, 0))
            two = jnp.where(rows == 0, edge[0:1, :], jnp.where(rows == 1, edge[1:2, :], pltpu.roll(now, 2, 0)))
            feats.append(
                taps[0, kind : kind + 1, span] * now
                + taps[1, kind : kind + 1, span] * one * clear
                + taps[2, kind : kind + 1, span] * two * clear_before
            )
        query[:, span] = feats[0]
        values = feats[1] * feats[2]
        product[:, span] = values

        group_rows = pl.ds(pl.multiple_of(tile * PER_TILE, PER_TILE), PER_TILE)
        rate = rates[group_rows, :]
        weight = weights[group_rows, :]
        total = jnp.zeros((PER_TILE, LANES), F32)
        leave_rows = []
        enter_rows = []
        for mode in range(MODES):
            r = jnp.broadcast_to(rate[:, mode : mode + 1], (PER_TILE, LANES))
            w = jnp.broadcast_to(weight[:, mode : mode + 1], (PER_TILE, LANES))
            total = total + w * jnp.exp(-r * apart)
            leave_rows.append(jnp.exp(-r * (LANES - 1.0 - offset)) * closing)
            enter_rows.append(w * jnp.exp(-r * (offset + 1.0)) * joined)
            whole = jnp.sum(jnp.exp(-r * LANES) * own, axis=0, keepdims=True)
            decay[4 * mode + tile // 2, pl.ds(tile % 2, 1), :] = whole
        lags[part * PER_TILE : (part + 1) * PER_TILE, :] = total
        high, low = halves(jnp.concatenate(enter_rows, axis=0).T)
        entering[part, :, :LANES] = high
        entering[part, :, LANES:] = low
        high, low = halves(jnp.concatenate(leave_rows, axis=0))
        states = split_dot(jnp.concatenate([high, low], axis=1), doubled(values))
        for mode in range(MODES):
            some = states[mode * PER_TILE : (mode + 1) * PER_TILE, :] * own
            fresh[4 * mode + tile // 2, pl.ds(tile % 2, 1), :] = jnp.sum(some, axis=0, keepdims=True)


def features(starts, lifetime, residues, qkv, rim, taps):
    chans = qkv.shape[2]
    tiles = chans // LANES
    width = FEATURE_TILES * LANES
    flat = pl.BlockSpec((LANES, width), lambda k: (0, k))
    small = pl.BlockSpec(lifetime.shape, lambda k: (0, 0))
    whole = pl.BlockSpec((8 * tiles, 2, LANES), lambda k: (0, 0, 0))
    return pl.pallas_call(
        features_kernel,
        grid=(chans // width,),
        in_specs=[
            SMEM,
            small,
            small,
            pl.BlockSpec((3, LANES, width), lambda k: (0, 0, k)),
            pl.BlockSpec((3, SHORT - 1, width), lambda k: (0, 0, k)),
            pl.BlockSpec((SHORT, 3, width), lambda k: (0, 0, k)),
        ],
        out_specs=[
            flat,
            flat,
            whole,
            pl.BlockSpec((FEATURE_TILES * PER_TILE, LANES), lambda k: (k, 0)),
            pl.BlockSpec((FEATURE_TILES, LANES, 2 * LANES), lambda k: (k, 0, 0)),
            whole,
        ],
        out_shape=[
            jax.ShapeDtypeStruct((LANES, chans), F32),
            jax.ShapeDtypeStruct((LANES, chans), F32),
            jax.ShapeDtypeStruct((8 * tiles, 2, LANES), F32),
            jax.ShapeDtypeStruct((tiles * PER_TILE, LANES), F32),
            jax.ShapeDtypeStruct((tiles, LANES, 2 * LANES), BF16),
            jax.ShapeDtypeStruct((8 * tiles, 2, LANES), F32),
        ],
        scratch_shapes=[pltpu.VMEM((LANES, LANES), F32), pltpu.VMEM((LANES, LANES), F32)],
        compiler_params=ROOMY,
        cost_estimate=pl.CostEstimate(flops=100_000_000, bytes_accessed=3_500_000, transcendentals=600_000),
        name="features",
    )(starts, lifetime, residues, qkv, rim, taps)


BASE_TILES = 2


def base_kernel(starts, lags, product, skip, base):
    first = lax.axis_index("seq") * LANES
    rows = iota((LANES, LANES), 0)
    cols = iota((LANES, LANES), 1)
    linked = (
        (segment_of(starts, first + rows) == segment_of(starts, first + cols)) & (rows >= cols)
    ).astype(F32)
    for part in range(BASE_TILES):
        span = slice(part * LANES, (part + 1) * LANES)
        values = product[:, span]
        both = doubled(values)
        total = skip[:, span] * values
        for group in range(PER_TILE):
            at = part * PER_TILE + group
            spread = jnp.broadcast_to(lags[at : at + 1, :], (LANES, LANES))
            rolled = pltpu.roll(spread, 0, 1, stride=1, stride_axis=0)
            high, low = halves(rolled * linked)
            out = split_dot(jnp.concatenate([high, low], axis=1), both)
            total = total + jnp.where(cols // GROUP == group, out, 0.0)
        base[:, span] = total


def base_work(starts, lags, product, skip):
    chans = product.shape[1]
    width = BASE_TILES * LANES
    flat = pl.BlockSpec((LANES, width), lambda k: (0, k))
    return pl.pallas_call(
        base_kernel,
        grid=(chans // width,),
        in_specs=[
            SMEM,
            pl.BlockSpec((BASE_TILES * PER_TILE, LANES), lambda k: (k, 0)),
            flat,
            pl.BlockSpec((1, width), lambda k: (0, k)),
        ],
        out_specs=flat,
        out_shape=jax.ShapeDtypeStruct((LANES, chans), F32),
        compiler_params=MODEST,
        cost_estimate=pl.CostEstimate(flops=1_100_000_000, bytes_accessed=1_100_000, transcendentals=0),
        name="base_work",
    )(starts, lags, product, skip)


def scan_kernel(starts, fresh, decay, entering):
    blocks = fresh.shape[0]
    whole = decay[lax.axis_index("seq")]
    gate = jnp.ones((blocks, 2, LANES), F32)
    number = iota((blocks, 2, LANES), 0)
    for j in range(1, starts.shape[0]):
        gate = jnp.where(number == starts[j] // LANES, 0.0, gate)
    state = jnp.zeros((2, LANES), F32)
    for block in range(blocks):
        entering[block] = state
        state = state * (whole * gate[block]) + fresh[block]


def scan_blocks(starts, fresh, decay):
    return pl.pallas_call(
        scan_kernel,
        in_specs=[SMEM, VMEM, VMEM],
        out_specs=VMEM,
        out_shape=jax.ShapeDtypeStruct(fresh.shape, F32),
        name="scan_blocks",
    )(starts, fresh, decay)


GATE_TILES = 4


def gate_kernel(entering, query, base, states, gated):
    own = own_group()
    for part in range(GATE_TILES):
        tile = pl.program_id(0) * GATE_TILES + part
        span = slice(part * LANES, (part + 1) * LANES)
        spread = []
        for mode in range(MODES):
            state = states[4 * mode + tile // 2, pl.ds(tile % 2, 1), :]
            spread.append(jnp.broadcast_to(state, (PER_TILE, LANES)) * own)
        carried = split_dot(entering[part], doubled(jnp.concatenate(spread, axis=0)))
        gated[:, span] = (query[:, span] * (base[:, span] + carried)).astype(BF16)


def gate(entering, query, base, states):
    chans = query.shape[1]
    width = GATE_TILES * LANES
    flat = pl.BlockSpec((LANES, width), lambda k: (0, k))
    return pl.pallas_call(
        gate_kernel,
        grid=(chans // width,),
        in_specs=[pl.BlockSpec((GATE_TILES, LANES, 2 * LANES), lambda k: (k, 0, 0)), flat, flat, VMEM],
        out_specs=flat,
        out_shape=jax.ShapeDtypeStruct((LANES, chans), BF16),
        compiler_params=MODEST,
        name="gate",
    )(entering, query, base, states)


def project_kernel(offsets, *refs):
    count = len(offsets)
    pieces, weight, rest = refs[:count], refs[count], refs[count + 1 :]
    held, sems = rest[-2:]
    mixed = rest[-3]
    planes = weight.shape[1]
    half = weight.shape[0] // 2
    here = lax.axis_index("seq") // weight.shape[0] - lax.axis_index("fsdp") + planes

    def copy(piece, part):
        some = pl.ds(part * half, half)
        plane = lax.rem(here - offsets[piece] + planes, planes)
        return pltpu.make_async_copy(weight.at[some, plane], held.at[piece, some], sems.at[piece, part])

    for piece in range(count):
        for part in range(2):
            copy(piece, part).start()
    depth = pieces[0].shape[1] // 2
    total = rest[0][...] if len(rest) == 4 else jnp.zeros(mixed.shape, F32)
    for piece in range(count):
        for part in range(2):
            copy(piece, part).wait()
            block = held[piece, part * half : (part + 1) * half].reshape(depth, mixed.shape[1])
            left = pieces[piece][:, part * depth : (part + 1) * depth]
            total = total + jnp.dot(left, block, preferred_element_type=F32)
    mixed[...] = total.astype(mixed.dtype)


def project(offsets, pieces, weight, earlier, dtype):
    outer, planes, rows, width = weight.shape
    tokens = pieces[0].shape[0]
    more = [] if earlier is None else [earlier]
    return pl.pallas_call(
        functools.partial(project_kernel, offsets),
        in_specs=[VMEM] * len(pieces) + [pl.BlockSpec(memory_space=pl.ANY)] + [VMEM] * len(more),
        out_specs=VMEM,
        out_shape=jax.ShapeDtypeStruct((tokens, width), dtype),
        scratch_shapes=[
            pltpu.VMEM((len(pieces), outer, rows, width), BF16),
            pltpu.SemaphoreType.DMA((len(pieces), 2)),
        ],
        compiler_params=MODEST,
        cost_estimate=pl.CostEstimate(
            flops=2 * tokens * outer * rows * width * len(pieces),
            bytes_accessed=2 * outer * rows * width * len(pieces),
            transcendentals=0,
        ),
        name="project",
    )(*pieces, weight, *more)


def shifted(x, axis, by):
    count = lax.axis_size(axis)
    return lax.ppermute(x, axis, [(i, (i + by) % count) for i in range(count)])


PLANES = 4


def on_device(qkv, short_taps, lifetime, residues, skip_gain, segment_starts, out_weight):
    kinds = jnp.transpose(qkv, (1, 0, 2))
    inner = lax.axis_size("seq") // PLANES
    edge, own_rows = lax.optimization_barrier((kinds[:, -(SHORT - 1) :, :], out_weight))
    arrived = [shifted(edge, "seq", 1)] + [shifted(own_rows, "seq", inner * j) for j in range(1, PLANES)]
    rim, *others = lax.optimization_barrier(arrived)
    column = jnp.concatenate([own_rows] + others, axis=0).reshape(PLANES, *out_weight.shape)
    groups = [list(range(x * inner, (x + 1) * inner)) for x in range(PLANES)]
    weight = lax.all_gather(column, "seq", axis=0, tiled=False, axis_index_groups=groups)

    query, product, fresh, lags, entering, decay = features(
        segment_starts, lifetime.T, residues.T, kinds, rim, short_taps
    )
    all_fresh = lax.all_to_all(fresh, "seq", 0, 0, tiled=True)
    base = base_work(segment_starts, lags, product, skip_gain[None, :])
    all_states = scan_blocks(segment_starts, all_fresh, decay)
    states = lax.all_to_all(all_states, "seq", 0, 0, tiled=True)
    gated = gate(entering, query, base, states)
    behind, ahead, across = (shifted(gated, "fsdp", by) for by in (1, 3, 2))
    total = project((0, 3, 1), [gated, behind, ahead], weight, None, F32)
    return project((2,), [across], weight, total, BF16)


def solution(mesh):
    return jax.shard_map(
        on_device,
        mesh=mesh,
        in_specs=(
            P(("dp", "seq"), None, "fsdp"),
            P(None, None, "fsdp"),
            P("fsdp", None),
            P("fsdp", None),
            P("fsdp"),
            P("dp"),
            P("seq", "fsdp"),
        ),
        out_specs=P(("dp", "seq"), "fsdp"),
        check_vma=False,
    )
```

```python
import functools

import jax
import jax.numpy as jnp
from jax import lax
from jax.experimental import pallas as pl
from jax.experimental.pallas import tpu as pltpu
from jax.sharding import PartitionSpec as P

GROUP = 16
MODES = 16
SHORT = 3
LANES = 128
PER_TILE = LANES // GROUP
F32 = jnp.float32
BF16 = jnp.bfloat16
ROOMY = pltpu.CompilerParams(vmem_limit_bytes=60 * 1024 * 1024)
MODEST = pltpu.CompilerParams(vmem_limit_bytes=24 * 1024 * 1024)
SMEM = pl.BlockSpec(memory_space=pltpu.SMEM)
VMEM = pl.BlockSpec(memory_space=pltpu.VMEM)


def iota(shape, axis):
    return lax.broadcasted_iota(jnp.int32, shape, axis)


def segment_of(starts, positions):
    total = jnp.zeros(positions.shape, jnp.int32)
    for j in range(1, starts.shape[0]):
        total = total + (positions >= starts[j]).astype(jnp.int32)
    return total


def not_start(starts, positions):
    clear = jnp.ones(positions.shape, F32)
    for j in range(starts.shape[0]):
        clear = jnp.where(positions == starts[j], 0.0, clear)
    return clear


def halves(x):
    high = x.astype(BF16)
    return high, (x - high.astype(F32)).astype(BF16)


def doubled(right):
    high, low = halves(right)
    upper = jnp.concatenate([high, low], axis=1)
    lower = jnp.concatenate([high, jnp.zeros_like(low)], axis=1)
    return jnp.concatenate([upper, lower], axis=0)


def split_dot(left, both):
    out = jnp.dot(left, both, preferred_element_type=F32)
    return out[:, :LANES] + out[:, LANES:]


def own_group():
    return (iota((PER_TILE, LANES), 0) == iota((PER_TILE, LANES), 1) // GROUP).astype(F32)


def turned(x):
    wide = jnp.concatenate([x, jnp.zeros((x.shape[0], LANES - x.shape[1]), F32)], axis=1)
    return jnp.concatenate([wide, jnp.zeros((LANES - x.shape[0], LANES), F32)], axis=0).T


FEATURE_TILES = 4


def features_kernel(
    starts, lifetime, qkv, rim, taps, query, product, fresh, decay, rates
):
    step = pl.program_id(0)
    first = lax.axis_index("seq") * LANES
    rows = iota((LANES, LANES), 0)
    own = own_group()

    @pl.when(step == 0)
    def _():
        rates[...] = turned(1.0 / lifetime[...])

    clear = not_start(starts, first + rows)
    clear_before = clear * not_start(starts, first + rows - 1)
    lane = iota((PER_TILE, LANES), 1)
    seg_lane = segment_of(starts, first + lane)
    last = segment_of(starts, jnp.full((PER_TILE, LANES), first + (LANES - 1)))
    closing = (seg_lane == last).astype(F32)
    offset = lane.astype(F32)

    for part in range(FEATURE_TILES):
        tile = step * FEATURE_TILES + part
        span = slice(part * LANES, (part + 1) * LANES)
        feats = []
        for kind in range(3):
            now = qkv[kind, :, span].astype(F32)
            edge = rim[kind, :, span].astype(F32)
            one = jnp.where(rows == 0, edge[1:2, :], pltpu.roll(now, 1, 0))
            two = jnp.where(rows == 0, edge[0:1, :], jnp.where(rows == 1, edge[1:2, :], pltpu.roll(now, 2, 0)))
            feats.append(
                taps[0, kind : kind + 1, span] * now
                + taps[1, kind : kind + 1, span] * one * clear
                + taps[2, kind : kind + 1, span] * two * clear_before
            )
        query[:, span] = feats[0]
        values = feats[1] * feats[2]
        product[:, span] = values

        group_rows = pl.ds(pl.multiple_of(tile * PER_TILE, PER_TILE), PER_TILE)
        rate = rates[group_rows, :]
        leave_rows = []
        for mode in range(MODES):
            r = jnp.broadcast_to(rate[:, mode : mode + 1], (PER_TILE, LANES))
            leave_rows.append(jnp.exp(-r * (LANES - 1.0 - offset)) * closing)
            whole = jnp.sum(jnp.exp(-r * LANES) * own, axis=0, keepdims=True)
            decay[4 * mode + tile // 2, pl.ds(tile % 2, 1), :] = whole
        high, low = halves(jnp.concatenate(leave_rows, axis=0))
        states = split_dot(jnp.concatenate([high, low], axis=1), doubled(values))
        for mode in range(MODES):
            some = states[mode * PER_TILE : (mode + 1) * PER_TILE, :] * own
            fresh[4 * mode + tile // 2, pl.ds(tile % 2, 1), :] = jnp.sum(some, axis=0, keepdims=True)


def features(starts, lifetime, qkv, rim, taps):
    chans = qkv.shape[2]
    tiles = chans // LANES
    width = FEATURE_TILES * LANES
    flat = pl.BlockSpec((LANES, width), lambda k: (0, k))
    small = pl.BlockSpec(lifetime.shape, lambda k: (0, 0))
    whole = pl.BlockSpec((8 * tiles, 2, LANES), lambda k: (0, 0, 0))
    return pl.pallas_call(
        features_kernel,
        grid=(chans // width,),
        in_specs=[
            SMEM,
            small,
            pl.BlockSpec((3, LANES, width), lambda k: (0, 0, k)),
            pl.BlockSpec((3, SHORT - 1, width), lambda k: (0, 0, k)),
            pl.BlockSpec((SHORT, 3, width), lambda k: (0, 0, k)),
        ],
        out_specs=[
            flat,
            flat,
            whole,
            whole,
        ],
        out_shape=[
            jax.ShapeDtypeStruct((LANES, chans), F32),
            jax.ShapeDtypeStruct((LANES, chans), F32),
            jax.ShapeDtypeStruct((8 * tiles, 2, LANES), F32),
            jax.ShapeDtypeStruct((8 * tiles, 2, LANES), F32),
        ],
        scratch_shapes=[pltpu.VMEM((LANES, LANES), F32)],
        compiler_params=ROOMY,
        cost_estimate=pl.CostEstimate(flops=100_000_000, bytes_accessed=2_500_000, transcendentals=200_000),
        name="features",
    )(starts, lifetime, qkv, rim, taps)


BASE_TILES = 2


def base_kernel(starts, lifetime, residues, product, skip, base, entering, rates, weights):
    step = pl.program_id(0)
    first = lax.axis_index("seq") * LANES
    rows = iota((LANES, LANES), 0)
    cols = iota((LANES, LANES), 1)

    @pl.when(step == 0)
    def _():
        rate = 1.0 / lifetime[...]
        double = 2.0 * rate
        series = double * (
            1.0
            - double
            * (0.5 - double * (1.0 / 6 - double * (1.0 / 24 - double * (1.0 / 120 - double * (1.0 / 720)))))
        )
        rates[...] = turned(rate)
        weights[...] = turned(residues[...] * jnp.sqrt(jnp.where(double < 0.07, series, 1.0 - jnp.exp(-double))))

    seg_col = segment_of(starts, first + cols)
    linked = ((segment_of(starts, first + rows) == seg_col) & (rows >= cols)).astype(F32)
    before = jnp.where(first > 0, segment_of(starts, jnp.full((PER_TILE, LANES), first - 1)), -1)
    joined = (seg_col[:PER_TILE] == before).astype(F32)
    lane = iota((PER_TILE, LANES), 1)
    offset = lane.astype(F32)
    apart = jnp.where(lane == 0, 0, LANES - lane).astype(F32)

    for part in range(BASE_TILES):
        tile = step * BASE_TILES + part
        group_rows = pl.ds(pl.multiple_of(tile * PER_TILE, PER_TILE), PER_TILE)
        rate = rates[group_rows, :]
        weight = weights[group_rows, :]
        lags = jnp.zeros((PER_TILE, LANES), F32)
        enter_rows = []
        for mode in range(MODES):
            r = jnp.broadcast_to(rate[:, mode : mode + 1], (PER_TILE, LANES))
            w = jnp.broadcast_to(weight[:, mode : mode + 1], (PER_TILE, LANES))
            lags = lags + w * jnp.exp(-r * apart)
            enter_rows.append(w * jnp.exp(-r * (offset + 1.0)) * joined)
        high, low = halves(jnp.concatenate(enter_rows, axis=0).T)
        entering[part, :, :LANES] = high
        entering[part, :, LANES:] = low

        span = slice(part * LANES, (part + 1) * LANES)
        values = product[:, span]
        both = doubled(values)
        total = skip[:, span] * values
        for group in range(PER_TILE):
            spread = jnp.broadcast_to(lags[group : group + 1, :], (LANES, LANES))
            rolled = pltpu.roll(spread, 0, 1, stride=1, stride_axis=0)
            high, low = halves(rolled * linked)
            out = split_dot(jnp.concatenate([high, low], axis=1), both)
            total = total + jnp.where(cols // GROUP == group, out, 0.0)
        base[:, span] = total


def base_work(starts, lifetime, residues, product, skip):
    chans = product.shape[1]
    tiles = chans // LANES
    width = BASE_TILES * LANES
    flat = pl.BlockSpec((LANES, width), lambda k: (0, k))
    small = pl.BlockSpec(lifetime.shape, lambda k: (0, 0))
    return pl.pallas_call(
        base_kernel,
        grid=(chans // width,),
        in_specs=[SMEM, small, small, flat, pl.BlockSpec((1, width), lambda k: (0, k))],
        out_specs=[flat, pl.BlockSpec((BASE_TILES, LANES, 2 * LANES), lambda k: (k, 0, 0))],
        out_shape=[
            jax.ShapeDtypeStruct((LANES, chans), F32),
            jax.ShapeDtypeStruct((tiles, LANES, 2 * LANES), BF16),
        ],
        scratch_shapes=[pltpu.VMEM((LANES, LANES), F32), pltpu.VMEM((LANES, LANES), F32)],
        compiler_params=MODEST,
        cost_estimate=pl.CostEstimate(flops=1_100_000_000, bytes_accessed=1_600_000, transcendentals=400_000),
        name="base_work",
    )(starts, lifetime, residues, product, skip)


def scan_kernel(starts, fresh, decay, entering):
    blocks = fresh.shape[0]
    whole = decay[lax.axis_index("seq")]
    gate = jnp.ones((blocks, 2, LANES), F32)
    number = iota((blocks, 2, LANES), 0)
    for j in range(1, starts.shape[0]):
        gate = jnp.where(number == starts[j] // LANES, 0.0, gate)
    state = jnp.zeros((2, LANES), F32)
    for block in range(blocks):
        entering[block] = state
        state = state * (whole * gate[block]) + fresh[block]


def scan_blocks(starts, fresh, decay):
    return pl.pallas_call(
        scan_kernel,
        in_specs=[SMEM, VMEM, VMEM],
        out_specs=VMEM,
        out_shape=jax.ShapeDtypeStruct(fresh.shape, F32),
        name="scan_blocks",
    )(starts, fresh, decay)


GATE_TILES = 4


def gate_kernel(entering, query, base, states, gated):
    own = own_group()
    for part in range(GATE_TILES):
        tile = pl.program_id(0) * GATE_TILES + part
        span = slice(part * LANES, (part + 1) * LANES)
        spread = []
        for mode in range(MODES):
            state = states[4 * mode + tile // 2, pl.ds(tile % 2, 1), :]
            spread.append(jnp.broadcast_to(state, (PER_TILE, LANES)) * own)
        carried = split_dot(entering[part], doubled(jnp.concatenate(spread, axis=0)))
        gated[:, span] = (query[:, span] * (base[:, span] + carried)).astype(BF16)


def gate(entering, query, base, states):
    chans = query.shape[1]
    width = GATE_TILES * LANES
    flat = pl.BlockSpec((LANES, width), lambda k: (0, k))
    return pl.pallas_call(
        gate_kernel,
        grid=(chans // width,),
        in_specs=[pl.BlockSpec((GATE_TILES, LANES, 2 * LANES), lambda k: (k, 0, 0)), flat, flat, VMEM],
        out_specs=flat,
        out_shape=jax.ShapeDtypeStruct((LANES, chans), BF16),
        compiler_params=MODEST,
        name="gate",
    )(entering, query, base, states)


def project_kernel(offsets, *refs):
    count = len(offsets)
    pieces, weight, rest = refs[:count], refs[count], refs[count + 1 :]
    held, sems = rest[-2:]
    mixed = rest[-3]
    planes = weight.shape[1]
    half = weight.shape[0] // 2
    here = lax.axis_index("seq") // weight.shape[0] - lax.axis_index("fsdp") + planes

    def copy(piece, part):
        some = pl.ds(part * half, half)
        plane = lax.rem(here - offsets[piece] + planes, planes)
        return pltpu.make_async_copy(weight.at[some, plane], held.at[piece, some], sems.at[piece, part])

    for piece in range(count):
        for part in range(2):
            copy(piece, part).start()
    depth = pieces[0].shape[1] // 2
    total = rest[0][...] if len(rest) == 4 else jnp.zeros(mixed.shape, F32)
    for piece in range(count):
        for part in range(2):
            copy(piece, part).wait()
            block = held[piece, part * half : (part + 1) * half].reshape(depth, mixed.shape[1])
            left = pieces[piece][:, part * depth : (part + 1) * depth]
            total = total + jnp.dot(left, block, preferred_element_type=F32)
    mixed[...] = total.astype(mixed.dtype)


def project(offsets, pieces, weight, earlier, dtype):
    outer, planes, rows, width = weight.shape
    tokens = pieces[0].shape[0]
    more = [] if earlier is None else [earlier]
    return pl.pallas_call(
        functools.partial(project_kernel, offsets),
        in_specs=[VMEM] * len(pieces) + [pl.BlockSpec(memory_space=pl.ANY)] + [VMEM] * len(more),
        out_specs=VMEM,
        out_shape=jax.ShapeDtypeStruct((tokens, width), dtype),
        scratch_shapes=[
            pltpu.VMEM((len(pieces), outer, rows, width), BF16),
            pltpu.SemaphoreType.DMA((len(pieces), 2)),
        ],
        compiler_params=MODEST,
        cost_estimate=pl.CostEstimate(
            flops=2 * tokens * outer * rows * width * len(pieces),
            bytes_accessed=2 * outer * rows * width * len(pieces),
            transcendentals=0,
        ),
        name="project",
    )(*pieces, weight, *more)


def shifted(x, axis, by):
    count = lax.axis_size(axis)
    return lax.ppermute(x, axis, [(i, (i + by) % count) for i in range(count)])


PLANES = 4


def on_device(qkv, short_taps, lifetime, residues, skip_gain, segment_starts, out_weight):
    kinds = jnp.transpose(qkv, (1, 0, 2))
    inner = lax.axis_size("seq") // PLANES
    edge, own_rows = lax.optimization_barrier((kinds[:, -(SHORT - 1) :, :], out_weight))
    arrived = [shifted(edge, "seq", 1)] + [shifted(own_rows, "seq", inner * j) for j in range(1, PLANES)]
    rim, *others = lax.optimization_barrier(arrived)
    column = jnp.concatenate([own_rows] + others, axis=0).reshape(PLANES, *out_weight.shape)
    groups = [list(range(x * inner, (x + 1) * inner)) for x in range(PLANES)]
    weight = lax.all_gather(column, "seq", axis=0, tiled=False, axis_index_groups=groups)

    query, product, fresh, decay = features(segment_starts, lifetime.T, kinds, rim, short_taps)
    all_fresh = lax.all_to_all(fresh, "seq", 0, 0, tiled=True)
    base, entering = base_work(segment_starts, lifetime.T, residues.T, product, skip_gain[None, :])
    all_states = scan_blocks(segment_starts, all_fresh, decay)
    states = lax.all_to_all(all_states, "seq", 0, 0, tiled=True)
    gated = gate(entering, query, base, states)
    behind, ahead, across = (shifted(gated, "fsdp", by) for by in (1, 3, 2))
    total = project((0, 2), [gated, across], weight, None, F32)
    return project((3, 1), [behind, ahead], weight, total, BF16)


def solution(mesh):
    return jax.shard_map(
        on_device,
        mesh=mesh,
        in_specs=(
            P(("dp", "seq"), None, "fsdp"),
            P(None, None, "fsdp"),
            P("fsdp", None),
            P("fsdp", None),
            P("fsdp"),
            P("dp"),
            P("seq", "fsdp"),
        ),
        out_specs=P(("dp", "seq"), "fsdp"),
        check_vma=False,
    )
```

```python
import functools

import jax
import jax.numpy as jnp
from jax import lax
from jax.experimental import pallas as pl
from jax.experimental.pallas import tpu as pltpu
from jax.sharding import PartitionSpec as P

GROUP = 16
MODES = 16
SHORT = 3
LANES = 128
PER_TILE = LANES // GROUP
F32 = jnp.float32
BF16 = jnp.bfloat16
ROOMY = pltpu.CompilerParams(vmem_limit_bytes=60 * 1024 * 1024)
MODEST = pltpu.CompilerParams(vmem_limit_bytes=24 * 1024 * 1024)
SMEM = pl.BlockSpec(memory_space=pltpu.SMEM)
VMEM = pl.BlockSpec(memory_space=pltpu.VMEM)


def iota(shape, axis):
    return lax.broadcasted_iota(jnp.int32, shape, axis)


def segment_of(starts, positions):
    total = jnp.zeros(positions.shape, jnp.int32)
    for j in range(1, starts.shape[0]):
        total = total + (positions >= starts[j]).astype(jnp.int32)
    return total


def not_start(starts, positions):
    clear = jnp.ones(positions.shape, F32)
    for j in range(starts.shape[0]):
        clear = jnp.where(positions == starts[j], 0.0, clear)
    return clear


def halves(x):
    high = x.astype(BF16)
    return high, (x - high.astype(F32)).astype(BF16)


def doubled(right):
    high, low = halves(right)
    upper = jnp.concatenate([high, low], axis=1)
    lower = jnp.concatenate([high, jnp.zeros_like(low)], axis=1)
    return jnp.concatenate([upper, lower], axis=0)


def split_dot(left, both):
    out = jnp.dot(left, both, preferred_element_type=F32)
    return out[:, :LANES] + out[:, LANES:]


def own_group():
    return (iota((PER_TILE, LANES), 0) == iota((PER_TILE, LANES), 1) // GROUP).astype(F32)


def turned(x):
    wide = jnp.concatenate([x, jnp.zeros((x.shape[0], LANES - x.shape[1]), F32)], axis=1)
    return jnp.concatenate([wide, jnp.zeros((LANES - x.shape[0], LANES), F32)], axis=0).T


FEATURE_TILES = 4


def features_kernel(
    starts, lifetime, qkv, rim, taps, query, product, fresh, decay, rates
):
    step = pl.program_id(0)
    first = lax.axis_index("seq") * LANES
    rows = iota((LANES, LANES), 0)
    own = own_group()

    @pl.when(step == 0)
    def _():
        rates[...] = turned(1.0 / lifetime[...])

    clear = not_start(starts, first + rows)
    clear_before = clear * not_start(starts, first + rows - 1)
    lane = iota((PER_TILE, LANES), 1)
    seg_lane = segment_of(starts, first + lane)
    last = segment_of(starts, jnp.full((PER_TILE, LANES), first + (LANES - 1)))
    closing = (seg_lane == last).astype(F32)
    offset = lane.astype(F32)

    for part in range(FEATURE_TILES):
        tile = step * FEATURE_TILES + part
        span = slice(part * LANES, (part + 1) * LANES)
        feats = []
        for kind in range(3):
            now = qkv[kind, :, span].astype(F32)
            edge = rim[kind, :, span].astype(F32)
            one = jnp.where(rows == 0, edge[1:2, :], pltpu.roll(now, 1, 0))
            two = jnp.where(rows == 0, edge[0:1, :], jnp.where(rows == 1, edge[1:2, :], pltpu.roll(now, 2, 0)))
            feats.append(
                taps[0, kind : kind + 1, span] * now
                + taps[1, kind : kind + 1, span] * one * clear
                + taps[2, kind : kind + 1, span] * two * clear_before
            )
        query[:, span] = feats[0]
        values = feats[1] * feats[2]
        product[:, span] = values

        group_rows = pl.ds(pl.multiple_of(tile * PER_TILE, PER_TILE), PER_TILE)
        rate = rates[group_rows, :]
        leave_rows = []
        for mode in range(MODES):
            r = jnp.broadcast_to(rate[:, mode : mode + 1], (PER_TILE, LANES))
            leave_rows.append(jnp.exp(-r * (LANES - 1.0 - offset)) * closing)
            whole = jnp.sum(jnp.exp(-r * LANES) * own, axis=0, keepdims=True)
            decay[4 * mode + tile // 2, pl.ds(tile % 2, 1), :] = whole
        high, low = halves(jnp.concatenate(leave_rows, axis=0))
        states = split_dot(jnp.concatenate([high, low], axis=1), doubled(values))
        for mode in range(MODES):
            some = states[mode * PER_TILE : (mode + 1) * PER_TILE, :] * own
            fresh[4 * mode + tile // 2, pl.ds(tile % 2, 1), :] = jnp.sum(some, axis=0, keepdims=True)


def features(starts, lifetime, qkv, rim, taps):
    chans = qkv.shape[2]
    tiles = chans // LANES
    width = FEATURE_TILES * LANES
    flat = pl.BlockSpec((LANES, width), lambda k: (0, k))
    small = pl.BlockSpec(lifetime.shape, lambda k: (0, 0))
    whole = pl.BlockSpec((8 * tiles, 2, LANES), lambda k: (0, 0, 0))
    return pl.pallas_call(
        features_kernel,
        grid=(chans // width,),
        in_specs=[
            SMEM,
            small,
            pl.BlockSpec((3, LANES, width), lambda k: (0, 0, k)),
            pl.BlockSpec((3, SHORT - 1, width), lambda k: (0, 0, k)),
            pl.BlockSpec((SHORT, 3, width), lambda k: (0, 0, k)),
        ],
        out_specs=[
            flat,
            flat,
            whole,
            whole,
        ],
        out_shape=[
            jax.ShapeDtypeStruct((LANES, chans), F32),
            jax.ShapeDtypeStruct((LANES, chans), F32),
            jax.ShapeDtypeStruct((8 * tiles, 2, LANES), F32),
            jax.ShapeDtypeStruct((8 * tiles, 2, LANES), F32),
        ],
        scratch_shapes=[pltpu.VMEM((LANES, LANES), F32)],
        compiler_params=ROOMY,
        cost_estimate=pl.CostEstimate(flops=100_000_000, bytes_accessed=2_500_000, transcendentals=200_000),
        name="features",
    )(starts, lifetime, qkv, rim, taps)


BASE_TILES = 2


def base_kernel(starts, lifetime, residues, product, skip, base, entering, rates, weights):
    step = pl.program_id(0)
    first = lax.axis_index("seq") * LANES
    rows = iota((LANES, LANES), 0)
    cols = iota((LANES, LANES), 1)

    @pl.when(step == 0)
    def _():
        rate = 1.0 / lifetime[...]
        double = 2.0 * rate
        series = double * (
            1.0
            - double
            * (0.5 - double * (1.0 / 6 - double * (1.0 / 24 - double * (1.0 / 120 - double * (1.0 / 720)))))
        )
        rates[...] = turned(rate)
        weights[...] = turned(residues[...] * jnp.sqrt(jnp.where(double < 0.07, series, 1.0 - jnp.exp(-double))))

    seg_col = segment_of(starts, first + cols)
    linked = ((segment_of(starts, first + rows) == seg_col) & (rows >= cols)).astype(F32)
    before = jnp.where(first > 0, segment_of(starts, jnp.full((PER_TILE, LANES), first - 1)), -1)
    joined = (seg_col[:PER_TILE] == before).astype(F32)
    lane = iota((PER_TILE, LANES), 1)
    offset = lane.astype(F32)
    apart = jnp.where(lane == 0, 0, LANES - lane).astype(F32)

    for part in range(BASE_TILES):
        tile = step * BASE_TILES + part
        group_rows = pl.ds(pl.multiple_of(tile * PER_TILE, PER_TILE), PER_TILE)
        rate = rates[group_rows, :]
        weight = weights[group_rows, :]
        lags = jnp.zeros((PER_TILE, LANES), F32)
        enter_rows = []
        for mode in range(MODES):
            r = jnp.broadcast_to(rate[:, mode : mode + 1], (PER_TILE, LANES))
            w = jnp.broadcast_to(weight[:, mode : mode + 1], (PER_TILE, LANES))
            lags = lags + w * jnp.exp(-r * apart)
            enter_rows.append(w * jnp.exp(-r * (offset + 1.0)) * joined)
        high, low = halves(jnp.concatenate(enter_rows, axis=0).T)
        entering[part, :, :LANES] = high
        entering[part, :, LANES:] = low

        span = slice(part * LANES, (part + 1) * LANES)
        values = product[:, span]
        both = doubled(values)
        total = skip[:, span] * values
        for group in range(PER_TILE):
            spread = jnp.broadcast_to(lags[group : group + 1, :], (LANES, LANES))
            rolled = pltpu.roll(spread, 0, 1, stride=1, stride_axis=0)
            high, low = halves(rolled * linked)
            out = split_dot(jnp.concatenate([high, low], axis=1), both)
            total = total + jnp.where(cols // GROUP == group, out, 0.0)
        base[:, span] = total


def base_work(starts, lifetime, residues, product, skip):
    chans = product.shape[1]
    tiles = chans // LANES
    width = BASE_TILES * LANES
    flat = pl.BlockSpec((LANES, width), lambda k: (0, k))
    small = pl.BlockSpec(lifetime.shape, lambda k: (0, 0))
    return pl.pallas_call(
        base_kernel,
        grid=(chans // width,),
        in_specs=[SMEM, small, small, flat, pl.BlockSpec((1, width), lambda k: (0, k))],
        out_specs=[flat, pl.BlockSpec((BASE_TILES, LANES, 2 * LANES), lambda k: (k, 0, 0))],
        out_shape=[
            jax.ShapeDtypeStruct((LANES, chans), F32),
            jax.ShapeDtypeStruct((tiles, LANES, 2 * LANES), BF16),
        ],
        scratch_shapes=[pltpu.VMEM((LANES, LANES), F32), pltpu.VMEM((LANES, LANES), F32)],
        compiler_params=MODEST,
        cost_estimate=pl.CostEstimate(flops=1_100_000_000, bytes_accessed=1_600_000, transcendentals=400_000),
        name="base_work",
    )(starts, lifetime, residues, product, skip)


def scan_kernel(starts, fresh, decay, entering):
    blocks = fresh.shape[0]
    whole = decay[lax.axis_index("seq")]
    gate = jnp.ones((blocks, 2, LANES), F32)
    number = iota((blocks, 2, LANES), 0)
    for j in range(1, starts.shape[0]):
        gate = jnp.where(number == starts[j] // LANES, 0.0, gate)
    state = jnp.zeros((2, LANES), F32)
    for block in range(blocks):
        entering[block] = state
        state = state * (whole * gate[block]) + fresh[block]


def scan_blocks(starts, fresh, decay):
    return pl.pallas_call(
        scan_kernel,
        in_specs=[SMEM, VMEM, VMEM],
        out_specs=VMEM,
        out_shape=jax.ShapeDtypeStruct(fresh.shape, F32),
        name="scan_blocks",
    )(starts, fresh, decay)


GATE_TILES = 4


def gate_kernel(entering, query, base, states, gated):
    own = own_group()
    for part in range(GATE_TILES):
        tile = pl.program_id(0) * GATE_TILES + part
        span = slice(part * LANES, (part + 1) * LANES)
        spread = []
        for mode in range(MODES):
            state = states[4 * mode + tile // 2, pl.ds(tile % 2, 1), :]
            spread.append(jnp.broadcast_to(state, (PER_TILE, LANES)) * own)
        carried = split_dot(entering[part], doubled(jnp.concatenate(spread, axis=0)))
        gated[:, span] = (query[:, span] * (base[:, span] + carried)).astype(BF16)


def gate(entering, query, base, states):
    chans = query.shape[1]
    width = GATE_TILES * LANES
    flat = pl.BlockSpec((LANES, width), lambda k: (0, k))
    return pl.pallas_call(
        gate_kernel,
        grid=(chans // width,),
        in_specs=[pl.BlockSpec((GATE_TILES, LANES, 2 * LANES), lambda k: (k, 0, 0)), flat, flat, VMEM],
        out_specs=flat,
        out_shape=jax.ShapeDtypeStruct((LANES, chans), BF16),
        compiler_params=MODEST,
        name="gate",
    )(entering, query, base, states)


def project_kernel(offsets, *refs):
    count = len(offsets)
    pieces, weight, rest = refs[:count], refs[count], refs[count + 1 :]
    held, sems = rest[-2:]
    mixed = rest[-3]
    planes = weight.shape[1]
    half = weight.shape[0] // 2
    here = lax.axis_index("fsdp")

    def copy(piece, part):
        some = pl.ds(part * half, half)
        plane = lax.rem(here + offsets[piece], planes)
        return pltpu.make_async_copy(weight.at[some, plane], held.at[piece, some], sems.at[piece, part])

    for piece in range(count):
        for part in range(2):
            copy(piece, part).start()
    depth = pieces[0].shape[1] // 2
    total = rest[0][...] if len(rest) == 4 else jnp.zeros(mixed.shape, F32)
    for piece in range(count):
        for part in range(2):
            copy(piece, part).wait()
            block = held[piece, part * half : (part + 1) * half].reshape(depth, mixed.shape[1])
            left = pieces[piece][:, part * depth : (part + 1) * depth]
            total = total + jnp.dot(left, block, preferred_element_type=F32)
    mixed[...] = total.astype(mixed.dtype)


def project(offsets, pieces, weight, earlier, dtype):
    outer, planes, rows, width = weight.shape
    tokens = pieces[0].shape[0]
    more = [] if earlier is None else [earlier]
    return pl.pallas_call(
        functools.partial(project_kernel, offsets),
        in_specs=[VMEM] * len(pieces) + [pl.BlockSpec(memory_space=pl.ANY)] + [VMEM] * len(more),
        out_specs=VMEM,
        out_shape=jax.ShapeDtypeStruct((tokens, width), dtype),
        scratch_shapes=[
            pltpu.VMEM((len(pieces), outer, rows, width), BF16),
            pltpu.SemaphoreType.DMA((len(pieces), 2)),
        ],
        compiler_params=MODEST,
        cost_estimate=pl.CostEstimate(
            flops=2 * tokens * outer * rows * width * len(pieces),
            bytes_accessed=2 * outer * rows * width * len(pieces),
            transcendentals=0,
        ),
        name="project",
    )(*pieces, weight, *more)


def shifted(x, axis, by):
    count = lax.axis_size(axis)
    return lax.ppermute(x, axis, [(i, (i + by) % count) for i in range(count)])


PLANES = 4


def on_device(qkv, short_taps, lifetime, residues, skip_gain, segment_starts, out_weight):
    kinds = jnp.transpose(qkv, (1, 0, 2))
    inner = lax.axis_size("seq") // PLANES
    rim = shifted(kinds[:, -(SHORT - 1) :, :], "seq", 1)
    lines = [list(range(j, lax.axis_size("seq"), inner)) for j in range(inner)]
    column = lax.all_gather(out_weight, "seq", axis=0, tiled=False, axis_index_groups=lines)
    rim, column = lax.optimization_barrier((rim, column))
    groups = [list(range(x * inner, (x + 1) * inner)) for x in range(PLANES)]
    weight = lax.all_gather(column, "seq", axis=0, tiled=False, axis_index_groups=groups)

    query, product, fresh, decay = features(segment_starts, lifetime.T, kinds, rim, short_taps)
    all_fresh = lax.all_to_all(fresh, "seq", 0, 0, tiled=True)
    base, entering = base_work(segment_starts, lifetime.T, residues.T, product, skip_gain[None, :])
    all_states = scan_blocks(segment_starts, all_fresh, decay)
    states = lax.all_to_all(all_states, "seq", 0, 0, tiled=True)
    gated = gate(entering, query, base, states)
    behind, ahead, across = (shifted(gated, "fsdp", by) for by in (1, 3, 2))
    total = project((0, 2), [gated, across], weight, None, F32)
    total = project((3,), [behind], weight, total, F32)
    return project((1,), [ahead], weight, total, BF16)


def solution(mesh):
    return jax.shard_map(
        on_device,
        mesh=mesh,
        in_specs=(
            P(("dp", "seq"), None, "fsdp"),
            P(None, None, "fsdp"),
            P("fsdp", None),
            P("fsdp", None),
            P("fsdp"),
            P("dp"),
            P("seq", "fsdp"),
        ),
        out_specs=P(("dp", "seq"), "fsdp"),
        check_vma=False,
    )
```

```python
import functools

import jax
import jax.numpy as jnp
from jax import lax
from jax.experimental import pallas as pl
from jax.experimental.pallas import tpu as pltpu
from jax.sharding import PartitionSpec as P

GROUP = 16
MODES = 16
SHORT = 3
LANES = 128
PER_TILE = LANES // GROUP
F32 = jnp.float32
BF16 = jnp.bfloat16
ROOMY = pltpu.CompilerParams(vmem_limit_bytes=59 * 1024 * 1024)
MODEST = pltpu.CompilerParams(vmem_limit_bytes=24 * 1024 * 1024)
SMEM = pl.BlockSpec(memory_space=pltpu.SMEM)
VMEM = pl.BlockSpec(memory_space=pltpu.VMEM)


def iota(shape, axis):
    return lax.broadcasted_iota(jnp.int32, shape, axis)


def segment_of(starts, positions):
    total = jnp.zeros(positions.shape, jnp.int32)
    for j in range(1, starts.shape[0]):
        total = total + (positions >= starts[j]).astype(jnp.int32)
    return total


def not_start(starts, positions):
    clear = jnp.ones(positions.shape, F32)
    for j in range(starts.shape[0]):
        clear = jnp.where(positions == starts[j], 0.0, clear)
    return clear


def halves(x):
    high = x.astype(BF16)
    return high, (x - high.astype(F32)).astype(BF16)


def doubled(right):
    high, low = halves(right)
    upper = jnp.concatenate([high, low], axis=1)
    lower = jnp.concatenate([high, jnp.zeros_like(low)], axis=1)
    return jnp.concatenate([upper, lower], axis=0)


def split_dot(left, both):
    out = jnp.dot(left, both, preferred_element_type=F32)
    return out[:, :LANES] + out[:, LANES:]


def own_group():
    return (iota((PER_TILE, LANES), 0) == iota((PER_TILE, LANES), 1) // GROUP).astype(F32)


def turned(x):
    wide = jnp.concatenate([x, jnp.zeros((x.shape[0], LANES - x.shape[1]), F32)], axis=1)
    return jnp.concatenate([wide, jnp.zeros((LANES - x.shape[0], LANES), F32)], axis=0).T


FEATURE_TILES = 4


def features_kernel(
    starts, lifetime, residues, skip, qkv, rim, taps, query, product, fresh, decay, aside, rates
):
    step = pl.program_id(0)
    first = lax.axis_index("seq") * LANES
    rows = iota((LANES, LANES), 0)
    own = own_group()

    @pl.when(step == 0)
    def _():
        rates[...] = turned(1.0 / lifetime[...])
        aside[...] = jnp.zeros(aside.shape, F32)
        aside[:MODES, : lifetime.shape[1]] = lifetime[...]
        aside[MODES : 2 * MODES, : residues.shape[1]] = residues[...]
        aside[2 * MODES :, :] = skip[...]

    clear = not_start(starts, first + rows)
    clear_before = clear * not_start(starts, first + rows - 1)
    lane = iota((PER_TILE, LANES), 1)
    seg_lane = segment_of(starts, first + lane)
    last = segment_of(starts, jnp.full((PER_TILE, LANES), first + (LANES - 1)))
    closing = (seg_lane == last).astype(F32)
    offset = lane.astype(F32)

    for part in range(FEATURE_TILES):
        tile = step * FEATURE_TILES + part
        span = slice(part * LANES, (part + 1) * LANES)
        feats = []
        for kind in range(3):
            now = qkv[kind, :, span].astype(F32)
            edge = rim[kind, :, span].astype(F32)
            one = jnp.where(rows == 0, edge[1:2, :], pltpu.roll(now, 1, 0))
            two = jnp.where(rows == 0, edge[0:1, :], jnp.where(rows == 1, edge[1:2, :], pltpu.roll(now, 2, 0)))
            feats.append(
                taps[0, kind : kind + 1, span] * now
                + taps[1, kind : kind + 1, span] * one * clear
                + taps[2, kind : kind + 1, span] * two * clear_before
            )
        query[:, span] = feats[0]
        values = feats[1] * feats[2]
        product[:, span] = values

        group_rows = pl.ds(pl.multiple_of(tile * PER_TILE, PER_TILE), PER_TILE)
        rate = rates[group_rows, :]
        leave_rows = []
        for mode in range(MODES):
            r = jnp.broadcast_to(rate[:, mode : mode + 1], (PER_TILE, LANES))
            leave_rows.append(jnp.exp(-r * (LANES - 1.0 - offset)) * closing)
            whole = jnp.sum(jnp.exp(-r * LANES) * own, axis=0, keepdims=True)
            decay[4 * mode + tile // 2, pl.ds(tile % 2, 1), :] = whole
        high, low = halves(jnp.concatenate(leave_rows, axis=0))
        states = split_dot(jnp.concatenate([high, low], axis=1), doubled(values))
        for mode in range(MODES):
            some = states[mode * PER_TILE : (mode + 1) * PER_TILE, :] * own
            fresh[4 * mode + tile // 2, pl.ds(tile % 2, 1), :] = jnp.sum(some, axis=0, keepdims=True)


def features(starts, lifetime, residues, skip, qkv, rim, taps):
    chans = qkv.shape[2]
    tiles = chans // LANES
    width = FEATURE_TILES * LANES
    flat = pl.BlockSpec((LANES, width), lambda k: (0, k))
    small = pl.BlockSpec(lifetime.shape, lambda k: (0, 0))
    whole = pl.BlockSpec((8 * tiles, 2, LANES), lambda k: (0, 0, 0))
    return pl.pallas_call(
        features_kernel,
        grid=(chans // width,),
        in_specs=[
            SMEM,
            small,
            small,
            pl.BlockSpec(skip.shape, lambda k: (0, 0)),
            pl.BlockSpec((3, LANES, width), lambda k: (0, 0, k)),
            pl.BlockSpec((3, SHORT - 1, width), lambda k: (0, 0, k)),
            pl.BlockSpec((SHORT, 3, width), lambda k: (0, 0, k)),
        ],
        out_specs=[
            flat,
            flat,
            whole,
            whole,
            pl.BlockSpec((2 * MODES + tiles, LANES), lambda k: (0, 0)),
        ],
        out_shape=[
            jax.ShapeDtypeStruct((LANES, chans), F32),
            jax.ShapeDtypeStruct((LANES, chans), F32),
            jax.ShapeDtypeStruct((8 * tiles, 2, LANES), F32),
            jax.ShapeDtypeStruct((8 * tiles, 2, LANES), F32),
            jax.ShapeDtypeStruct((2 * MODES + tiles, LANES), F32),
        ],
        scratch_shapes=[pltpu.VMEM((LANES, LANES), F32)],
        compiler_params=ROOMY,
        cost_estimate=pl.CostEstimate(flops=100_000_000, bytes_accessed=2_500_000, transcendentals=200_000),
        name="features",
    )(starts, lifetime, residues, skip, qkv, rim, taps)


BASE_TILES = 2


def base_kernel(starts, aside, product, query, base, entering, same_query, rates, weights):
    step = pl.program_id(0)
    first = lax.axis_index("seq") * LANES
    rows = iota((LANES, LANES), 0)
    cols = iota((LANES, LANES), 1)

    @pl.when(step == 0)
    def _():
        groups = product.shape[1] * pl.num_programs(0) // GROUP
        rate = 1.0 / aside[:MODES, :groups]
        double = 2.0 * rate
        series = double * (
            1.0
            - double
            * (0.5 - double * (1.0 / 6 - double * (1.0 / 24 - double * (1.0 / 120 - double * (1.0 / 720)))))
        )
        rates[...] = turned(rate)
        weights[...] = turned(aside[MODES : 2 * MODES, :groups] * jnp.sqrt(jnp.where(double < 0.07, series, 1.0 - jnp.exp(-double))))

    seg_col = segment_of(starts, first + cols)
    linked = ((segment_of(starts, first + rows) == seg_col) & (rows >= cols)).astype(F32)
    before = jnp.where(first > 0, segment_of(starts, jnp.full((PER_TILE, LANES), first - 1)), -1)
    joined = (seg_col[:PER_TILE] == before).astype(F32)
    lane = iota((PER_TILE, LANES), 1)
    offset = lane.astype(F32)
    apart = jnp.where(lane == 0, 0, LANES - lane).astype(F32)

    for part in range(BASE_TILES):
        tile = step * BASE_TILES + part
        group_rows = pl.ds(pl.multiple_of(tile * PER_TILE, PER_TILE), PER_TILE)
        rate = rates[group_rows, :]
        weight = weights[group_rows, :]
        lags = jnp.zeros((PER_TILE, LANES), F32)
        enter_rows = []
        for mode in range(MODES):
            r = jnp.broadcast_to(rate[:, mode : mode + 1], (PER_TILE, LANES))
            w = jnp.broadcast_to(weight[:, mode : mode + 1], (PER_TILE, LANES))
            lags = lags + w * jnp.exp(-r * apart)
            enter_rows.append(w * jnp.exp(-r * (offset + 1.0)) * joined)
        high, low = halves(jnp.concatenate(enter_rows, axis=0).T)
        entering[part, :, :LANES] = high
        entering[part, :, LANES:] = low

        span = slice(part * LANES, (part + 1) * LANES)
        values = product[:, span]
        both = doubled(values)
        total = aside[pl.ds(2 * MODES + tile, 1), :] * values
        for group in range(PER_TILE):
            spread = jnp.broadcast_to(lags[group : group + 1, :], (LANES, LANES))
            rolled = pltpu.roll(spread, 0, 1, stride=1, stride_axis=0)
            high, low = halves(rolled * linked)
            out = split_dot(jnp.concatenate([high, low], axis=1), both)
            total = total + jnp.where(cols // GROUP == group, out, 0.0)
        base[:, span] = total
    same_query[...] = query[...]


def base_work(starts, aside, product, query):
    chans = product.shape[1]
    tiles = chans // LANES
    width = BASE_TILES * LANES
    flat = pl.BlockSpec((LANES, width), lambda k: (0, k))
    return pl.pallas_call(
        base_kernel,
        grid=(chans // width,),
        in_specs=[SMEM, pl.BlockSpec(aside.shape, lambda k: (0, 0)), flat, flat],
        out_specs=[flat, pl.BlockSpec((BASE_TILES, LANES, 2 * LANES), lambda k: (k, 0, 0)), flat],
        out_shape=[
            jax.ShapeDtypeStruct((LANES, chans), F32),
            jax.ShapeDtypeStruct((tiles, LANES, 2 * LANES), BF16),
            jax.ShapeDtypeStruct((LANES, chans), F32),
        ],
        scratch_shapes=[pltpu.VMEM((LANES, LANES), F32), pltpu.VMEM((LANES, LANES), F32)],
        compiler_params=MODEST,
        cost_estimate=pl.CostEstimate(flops=1_100_000_000, bytes_accessed=1_600_000, transcendentals=400_000),
        name="base_work",
    )(starts, aside, product, query)


def scan_kernel(starts, fresh, decay, entering):
    blocks = fresh.shape[0]
    whole = decay[lax.axis_index("seq")]
    gate = jnp.ones((blocks, 2, LANES), F32)
    number = iota((blocks, 2, LANES), 0)
    for j in range(1, starts.shape[0]):
        gate = jnp.where(number == starts[j] // LANES, 0.0, gate)
    state = jnp.zeros((2, LANES), F32)
    for block in range(blocks):
        entering[block] = state
        state = state * (whole * gate[block]) + fresh[block]


def scan_blocks(starts, fresh, decay):
    return pl.pallas_call(
        scan_kernel,
        in_specs=[SMEM, VMEM, VMEM],
        out_specs=VMEM,
        out_shape=jax.ShapeDtypeStruct(fresh.shape, F32),
        name="scan_blocks",
    )(starts, fresh, decay)


GATE_TILES = 4


def gate_kernel(entering, query, base, states, gated):
    own = own_group()
    for part in range(GATE_TILES):
        tile = pl.program_id(0) * GATE_TILES + part
        span = slice(part * LANES, (part + 1) * LANES)
        spread = []
        for mode in range(MODES):
            state = states[4 * mode + tile // 2, pl.ds(tile % 2, 1), :]
            spread.append(jnp.broadcast_to(state, (PER_TILE, LANES)) * own)
        carried = split_dot(entering[part], doubled(jnp.concatenate(spread, axis=0)))
        gated[:, span] = (query[:, span] * (base[:, span] + carried)).astype(BF16)


def gate(entering, query, base, states):
    chans = query.shape[1]
    width = GATE_TILES * LANES
    flat = pl.BlockSpec((LANES, width), lambda k: (0, k))
    return pl.pallas_call(
        gate_kernel,
        grid=(chans // width,),
        in_specs=[pl.BlockSpec((GATE_TILES, LANES, 2 * LANES), lambda k: (k, 0, 0)), flat, flat, VMEM],
        out_specs=flat,
        out_shape=jax.ShapeDtypeStruct((LANES, chans), BF16),
        compiler_params=MODEST,
        name="gate",
    )(entering, query, base, states)


def project_kernel(offsets, *refs):
    count = len(offsets)
    pieces, weight, rest = refs[:count], refs[count], refs[count + 1 :]
    held, sems = rest[-2:]
    mixed = rest[-3]
    planes = weight.shape[1]
    half = weight.shape[0] // 2
    here = lax.axis_index("fsdp")

    def copy(piece, part):
        some = pl.ds(part * half, half)
        plane = lax.rem(here + offsets[piece], planes)
        return pltpu.make_async_copy(weight.at[some, plane], held.at[piece, some], sems.at[piece, part])

    for piece in range(count):
        for part in range(2):
            copy(piece, part).start()
    depth = pieces[0].shape[1] // 2
    total = rest[0][...] if len(rest) == 4 else jnp.zeros(mixed.shape, F32)
    for piece in range(count):
        for part in range(2):
            copy(piece, part).wait()
            block = held[piece, part * half : (part + 1) * half].reshape(depth, mixed.shape[1])
            left = pieces[piece][:, part * depth : (part + 1) * depth]
            total = total + jnp.dot(left, block, preferred_element_type=F32)
    mixed[...] = total.astype(mixed.dtype)


def project(offsets, pieces, weight, earlier, dtype):
    outer, planes, rows, width = weight.shape
    tokens = pieces[0].shape[0]
    more = [] if earlier is None else [earlier]
    return pl.pallas_call(
        functools.partial(project_kernel, offsets),
        in_specs=[VMEM] * len(pieces) + [pl.BlockSpec(memory_space=pl.ANY)] + [VMEM] * len(more),
        out_specs=VMEM,
        out_shape=jax.ShapeDtypeStruct((tokens, width), dtype),
        scratch_shapes=[
            pltpu.VMEM((len(pieces), outer, rows, width), BF16),
            pltpu.SemaphoreType.DMA((len(pieces), 2)),
        ],
        compiler_params=MODEST,
        cost_estimate=pl.CostEstimate(
            flops=2 * tokens * outer * rows * width * len(pieces),
            bytes_accessed=2 * outer * rows * width * len(pieces),
            transcendentals=0,
        ),
        name="project",
    )(*pieces, weight, *more)


def shifted(x, axis, by):
    count = lax.axis_size(axis)
    return lax.ppermute(x, axis, [(i, (i + by) % count) for i in range(count)])


PLANES = 4


def on_device(qkv, short_taps, lifetime, residues, skip_gain, segment_starts, out_weight):
    kinds = jnp.transpose(qkv, (1, 0, 2))
    inner = lax.axis_size("seq") // PLANES
    rim = shifted(kinds[:, -(SHORT - 1) :, :], "seq", 1)
    lines = [list(range(j, lax.axis_size("seq"), inner)) for j in range(inner)]
    column = lax.all_gather(out_weight, "seq", axis=0, tiled=False, axis_index_groups=lines)
    rim, column = lax.optimization_barrier((rim, column))
    groups = [list(range(x * inner, (x + 1) * inner)) for x in range(PLANES)]
    weight = lax.all_gather(column, "seq", axis=0, tiled=False, axis_index_groups=groups)

    query, product, fresh, decay, aside = features(
        segment_starts, lifetime.T, residues.T, skip_gain.reshape(-1, LANES), kinds, rim, short_taps
    )
    all_fresh = lax.all_to_all(fresh, "seq", 0, 0, tiled=True)
    base, entering, query = base_work(segment_starts, aside, product, query)
    all_states = scan_blocks(segment_starts, all_fresh, decay)
    states = lax.all_to_all(all_states, "seq", 0, 0, tiled=True)
    gated = gate(entering, query, base, states)
    behind, ahead, across = (shifted(gated, "fsdp", by) for by in (1, 3, 2))
    total = project((0, 2), [gated, across], weight, None, F32)
    total = project((3,), [behind], weight, total, F32)
    return project((1,), [ahead], weight, total, BF16)


def solution(mesh):
    return jax.shard_map(
        on_device,
        mesh=mesh,
        in_specs=(
            P(("dp", "seq"), None, "fsdp"),
            P(None, None, "fsdp"),
            P("fsdp", None),
            P("fsdp", None),
            P("fsdp"),
            P("dp"),
            P("seq", "fsdp"),
        ),
        out_specs=P(("dp", "seq"), "fsdp"),
        check_vma=False,
    )
```

```python
import functools

import jax
import jax.numpy as jnp
from jax import lax
from jax.experimental import pallas as pl
from jax.experimental.pallas import tpu as pltpu
from jax.sharding import PartitionSpec as P

GROUP = 16
MODES = 16
SHORT = 3
LANES = 128
PER_TILE = LANES // GROUP
F32 = jnp.float32
BF16 = jnp.bfloat16
ROOMY = pltpu.CompilerParams(vmem_limit_bytes=59 * 1024 * 1024)
MODEST = pltpu.CompilerParams(vmem_limit_bytes=24 * 1024 * 1024)
SMEM = pl.BlockSpec(memory_space=pltpu.SMEM)
VMEM = pl.BlockSpec(memory_space=pltpu.VMEM)


def iota(shape, axis):
    return lax.broadcasted_iota(jnp.int32, shape, axis)


def segment_of(starts, positions):
    total = jnp.zeros(positions.shape, jnp.int32)
    for j in range(1, starts.shape[0]):
        total = total + (positions >= starts[j]).astype(jnp.int32)
    return total


def not_start(starts, positions):
    clear = jnp.ones(positions.shape, F32)
    for j in range(starts.shape[0]):
        clear = jnp.where(positions == starts[j], 0.0, clear)
    return clear


def halves(x):
    high = x.astype(BF16)
    return high, (x - high.astype(F32)).astype(BF16)


def doubled(right):
    high, low = halves(right)
    upper = jnp.concatenate([high, low], axis=1)
    lower = jnp.concatenate([high, jnp.zeros_like(low)], axis=1)
    return jnp.concatenate([upper, lower], axis=0)


def split_dot(left, both):
    out = jnp.dot(left, both, preferred_element_type=F32)
    return out[:, :LANES] + out[:, LANES:]


def own_group():
    return (iota((PER_TILE, LANES), 0) == iota((PER_TILE, LANES), 1) // GROUP).astype(F32)


def turned(x):
    wide = jnp.concatenate([x, jnp.zeros((x.shape[0], LANES - x.shape[1]), F32)], axis=1)
    return jnp.concatenate([wide, jnp.zeros((LANES - x.shape[0], LANES), F32)], axis=0).T


FEATURE_TILES = 4


def features_kernel(
    starts, lifetime, residues, skip, qkv, rim, taps, query, product, fresh, decay, aside, rates
):
    step = pl.program_id(0)
    first = lax.axis_index("seq") * LANES
    rows = iota((LANES, LANES), 0)
    own = own_group()

    @pl.when(step == 0)
    def _():
        rates[...] = turned(1.0 / lifetime[...])
        aside[...] = jnp.zeros(aside.shape, F32)
        aside[:MODES, : lifetime.shape[1]] = lifetime[...]
        aside[MODES : 2 * MODES, : residues.shape[1]] = residues[...]
        aside[2 * MODES :, :] = skip[...]

    clear = not_start(starts, first + rows)
    clear_before = clear * not_start(starts, first + rows - 1)
    lane = iota((PER_TILE, LANES), 1)
    seg_lane = segment_of(starts, first + lane)
    last = segment_of(starts, jnp.full((PER_TILE, LANES), first + (LANES - 1)))
    closing = (seg_lane == last).astype(F32)
    offset = lane.astype(F32)

    for part in range(FEATURE_TILES):
        tile = step * FEATURE_TILES + part
        span = slice(part * LANES, (part + 1) * LANES)
        feats = []
        for kind in range(3):
            now = qkv[kind, :, span].astype(F32)
            edge = rim[kind, :, span].astype(F32)
            one = jnp.where(rows == 0, edge[1:2, :], pltpu.roll(now, 1, 0))
            two = jnp.where(rows == 0, edge[0:1, :], jnp.where(rows == 1, edge[1:2, :], pltpu.roll(now, 2, 0)))
            feats.append(
                taps[0, kind : kind + 1, span] * now
                + taps[1, kind : kind + 1, span] * one * clear
                + taps[2, kind : kind + 1, span] * two * clear_before
            )
        query[:, span] = feats[0]
        values = feats[1] * feats[2]
        product[:, span] = values

        group_rows = pl.ds(pl.multiple_of(tile * PER_TILE, PER_TILE), PER_TILE)
        rate = rates[group_rows, :]
        leave_rows = []
        for mode in range(MODES):
            r = jnp.broadcast_to(rate[:, mode : mode + 1], (PER_TILE, LANES))
            leave_rows.append(jnp.exp(-r * (LANES - 1.0 - offset)) * closing)
            whole = jnp.sum(jnp.exp(-r * LANES) * own, axis=0, keepdims=True)
            decay[4 * mode + tile // 2, pl.ds(tile % 2, 1), :] = whole
        high, low = halves(jnp.concatenate(leave_rows, axis=0))
        states = split_dot(jnp.concatenate([high, low], axis=1), doubled(values))
        for mode in range(MODES):
            some = states[mode * PER_TILE : (mode + 1) * PER_TILE, :] * own
            fresh[4 * mode + tile // 2, pl.ds(tile % 2, 1), :] = jnp.sum(some, axis=0, keepdims=True)


def features(starts, lifetime, residues, skip, qkv, rim, taps):
    chans = qkv.shape[2]
    tiles = chans // LANES
    width = FEATURE_TILES * LANES
    flat = pl.BlockSpec((LANES, width), lambda k: (0, k))
    small = pl.BlockSpec(lifetime.shape, lambda k: (0, 0))
    whole = pl.BlockSpec((8 * tiles, 2, LANES), lambda k: (0, 0, 0))
    return pl.pallas_call(
        features_kernel,
        grid=(chans // width,),
        in_specs=[
            SMEM,
            small,
            small,
            pl.BlockSpec(skip.shape, lambda k: (0, 0)),
            pl.BlockSpec((3, LANES, width), lambda k: (0, 0, k)),
            pl.BlockSpec((3, SHORT - 1, width), lambda k: (0, 0, k)),
            pl.BlockSpec((SHORT, 3, width), lambda k: (0, 0, k)),
        ],
        out_specs=[
            flat,
            flat,
            whole,
            whole,
            pl.BlockSpec((2 * MODES + tiles, LANES), lambda k: (0, 0)),
        ],
        out_shape=[
            jax.ShapeDtypeStruct((LANES, chans), F32),
            jax.ShapeDtypeStruct((LANES, chans), F32),
            jax.ShapeDtypeStruct((8 * tiles, 2, LANES), F32),
            jax.ShapeDtypeStruct((8 * tiles, 2, LANES), F32),
            jax.ShapeDtypeStruct((2 * MODES + tiles, LANES), F32),
        ],
        scratch_shapes=[pltpu.VMEM((LANES, LANES), F32)],
        compiler_params=ROOMY,
        cost_estimate=pl.CostEstimate(flops=100_000_000, bytes_accessed=2_500_000, transcendentals=200_000),
        name="features",
    )(starts, lifetime, residues, skip, qkv, rim, taps)


BASE_TILES = 4


def base_kernel(starts, aside, product, query, base, entering, same_query, rates, weights):
    step = pl.program_id(0)
    first = lax.axis_index("seq") * LANES
    rows = iota((LANES, LANES), 0)
    cols = iota((LANES, LANES), 1)

    @pl.when(step == 0)
    def _():
        groups = product.shape[1] * pl.num_programs(0) // GROUP
        rate = 1.0 / aside[:MODES, :groups]
        double = 2.0 * rate
        series = double * (
            1.0
            - double
            * (0.5 - double * (1.0 / 6 - double * (1.0 / 24 - double * (1.0 / 120 - double * (1.0 / 720)))))
        )
        rates[...] = turned(rate)
        weights[...] = turned(aside[MODES : 2 * MODES, :groups] * jnp.sqrt(jnp.where(double < 0.07, series, 1.0 - jnp.exp(-double))))

    seg_col = segment_of(starts, first + cols)
    linked = ((segment_of(starts, first + rows) == seg_col) & (rows >= cols)).astype(F32)
    before = jnp.where(first > 0, segment_of(starts, jnp.full((PER_TILE, LANES), first - 1)), -1)
    joined = (seg_col[:PER_TILE] == before).astype(F32)
    lane = iota((PER_TILE, LANES), 1)
    offset = lane.astype(F32)
    apart = jnp.where(lane == 0, 0, LANES - lane).astype(F32)

    for part in range(BASE_TILES):
        tile = step * BASE_TILES + part
        group_rows = pl.ds(pl.multiple_of(tile * PER_TILE, PER_TILE), PER_TILE)
        rate = rates[group_rows, :]
        weight = weights[group_rows, :]
        lags = jnp.zeros((PER_TILE, LANES), F32)
        enter_rows = []
        for mode in range(MODES):
            r = jnp.broadcast_to(rate[:, mode : mode + 1], (PER_TILE, LANES))
            w = jnp.broadcast_to(weight[:, mode : mode + 1], (PER_TILE, LANES))
            lags = lags + w * jnp.exp(-r * apart)
            enter_rows.append(w * jnp.exp(-r * (offset + 1.0)) * joined)
        high, low = halves(jnp.concatenate(enter_rows, axis=0).T)
        entering[part, :, :LANES] = high
        entering[part, :, LANES:] = low

        span = slice(part * LANES, (part + 1) * LANES)
        values = product[:, span]
        both = doubled(values)
        total = aside[pl.ds(2 * MODES + tile, 1), :] * values
        for group in range(PER_TILE):
            spread = jnp.broadcast_to(lags[group : group + 1, :], (LANES, LANES))
            rolled = pltpu.roll(spread, 0, 1, stride=1, stride_axis=0)
            high, low = halves(rolled * linked)
            out = split_dot(jnp.concatenate([high, low], axis=1), both)
            total = total + jnp.where(cols // GROUP == group, out, 0.0)
        base[:, span] = total
    same_query[...] = query[...]


def base_work(starts, aside, product, query):
    chans = product.shape[1]
    tiles = chans // LANES
    width = BASE_TILES * LANES
    flat = pl.BlockSpec((LANES, width), lambda k: (0, k))
    return pl.pallas_call(
        base_kernel,
        grid=(chans // width,),
        in_specs=[SMEM, pl.BlockSpec(aside.shape, lambda k: (0, 0)), flat, flat],
        out_specs=[flat, pl.BlockSpec((BASE_TILES, LANES, 2 * LANES), lambda k: (k, 0, 0)), flat],
        out_shape=[
            jax.ShapeDtypeStruct((LANES, chans), F32),
            jax.ShapeDtypeStruct((tiles, LANES, 2 * LANES), BF16),
            jax.ShapeDtypeStruct((LANES, chans), F32),
        ],
        scratch_shapes=[pltpu.VMEM((LANES, LANES), F32), pltpu.VMEM((LANES, LANES), F32)],
        compiler_params=MODEST,
        cost_estimate=pl.CostEstimate(flops=1_100_000_000, bytes_accessed=1_600_000, transcendentals=400_000),
        name="base_work",
    )(starts, aside, product, query)


def scan_kernel(starts, fresh, decay, entering):
    blocks = fresh.shape[0]
    whole = decay[lax.axis_index("seq")]
    gate = jnp.ones((blocks, 2, LANES), F32)
    number = iota((blocks, 2, LANES), 0)
    for j in range(1, starts.shape[0]):
        gate = jnp.where(number == starts[j] // LANES, 0.0, gate)
    state = jnp.zeros((2, LANES), F32)
    for block in range(blocks):
        entering[block] = state
        state = state * (whole * gate[block]) + fresh[block]


def scan_blocks(starts, fresh, decay):
    return pl.pallas_call(
        scan_kernel,
        in_specs=[SMEM, VMEM, VMEM],
        out_specs=VMEM,
        out_shape=jax.ShapeDtypeStruct(fresh.shape, F32),
        name="scan_blocks",
    )(starts, fresh, decay)


GATE_TILES = 8


def gate_kernel(entering, query, base, states, gated):
    own = own_group()
    for part in range(GATE_TILES):
        tile = pl.program_id(0) * GATE_TILES + part
        span = slice(part * LANES, (part + 1) * LANES)
        spread = []
        for mode in range(MODES):
            state = states[4 * mode + tile // 2, pl.ds(tile % 2, 1), :]
            spread.append(jnp.broadcast_to(state, (PER_TILE, LANES)) * own)
        carried = split_dot(entering[part], doubled(jnp.concatenate(spread, axis=0)))
        gated[:, span] = (query[:, span] * (base[:, span] + carried)).astype(BF16)


def gate(entering, query, base, states):
    chans = query.shape[1]
    width = GATE_TILES * LANES
    flat = pl.BlockSpec((LANES, width), lambda k: (0, k))
    return pl.pallas_call(
        gate_kernel,
        grid=(chans // width,),
        in_specs=[pl.BlockSpec((GATE_TILES, LANES, 2 * LANES), lambda k: (k, 0, 0)), flat, flat, VMEM],
        out_specs=flat,
        out_shape=jax.ShapeDtypeStruct((LANES, chans), BF16),
        compiler_params=MODEST,
        name="gate",
    )(entering, query, base, states)


def project_kernel(offsets, *refs):
    count = len(offsets)
    pieces, weight, rest = refs[:count], refs[count], refs[count + 1 :]
    held, sems = rest[-2:]
    mixed = rest[-3]
    planes = weight.shape[1]
    half = weight.shape[0] // 2
    here = lax.axis_index("fsdp")

    def copy(piece, part):
        some = pl.ds(part * half, half)
        plane = lax.rem(here + offsets[piece], planes)
        return pltpu.make_async_copy(weight.at[some, plane], held.at[piece, some], sems.at[piece, part])

    for piece in range(count):
        for part in range(2):
            copy(piece, part).start()
    depth = pieces[0].shape[1] // 2
    total = rest[0][...] if len(rest) == 4 else jnp.zeros(mixed.shape, F32)
    for piece in range(count):
        for part in range(2):
            copy(piece, part).wait()
            block = held[piece, part * half : (part + 1) * half].reshape(depth, mixed.shape[1])
            left = pieces[piece][:, part * depth : (part + 1) * depth]
            total = total + jnp.dot(left, block, preferred_element_type=F32)
    mixed[...] = total.astype(mixed.dtype)


def project(offsets, pieces, weight, earlier, dtype):
    outer, planes, rows, width = weight.shape
    tokens = pieces[0].shape[0]
    more = [] if earlier is None else [earlier]
    return pl.pallas_call(
        functools.partial(project_kernel, offsets),
        in_specs=[VMEM] * len(pieces) + [pl.BlockSpec(memory_space=pl.ANY)] + [VMEM] * len(more),
        out_specs=VMEM,
        out_shape=jax.ShapeDtypeStruct((tokens, width), dtype),
        scratch_shapes=[
            pltpu.VMEM((len(pieces), outer, rows, width), BF16),
            pltpu.SemaphoreType.DMA((len(pieces), 2)),
        ],
        compiler_params=MODEST,
        cost_estimate=pl.CostEstimate(
            flops=2 * tokens * outer * rows * width * len(pieces),
            bytes_accessed=2 * outer * rows * width * len(pieces),
            transcendentals=0,
        ),
        name="project",
    )(*pieces, weight, *more)


def shifted(x, axis, by):
    count = lax.axis_size(axis)
    return lax.ppermute(x, axis, [(i, (i + by) % count) for i in range(count)])


PLANES = 4


def on_device(qkv, short_taps, lifetime, residues, skip_gain, segment_starts, out_weight):
    kinds = jnp.transpose(qkv, (1, 0, 2))
    inner = lax.axis_size("seq") // PLANES
    rim = shifted(kinds[:, -(SHORT - 1) :, :], "seq", 1)
    lines = [list(range(j, lax.axis_size("seq"), inner)) for j in range(inner)]
    column = lax.all_gather(out_weight, "seq", axis=0, tiled=False, axis_index_groups=lines)
    rim, column = lax.optimization_barrier((rim, column))
    groups = [list(range(x * inner, (x + 1) * inner)) for x in range(PLANES)]
    weight = lax.all_gather(column, "seq", axis=0, tiled=False, axis_index_groups=groups)

    query, product, fresh, decay, aside = features(
        segment_starts, lifetime.T, residues.T, skip_gain.reshape(-1, LANES), kinds, rim, short_taps
    )
    all_fresh = lax.all_to_all(fresh, "seq", 0, 0, tiled=True)
    base, entering, query = base_work(segment_starts, aside, product, query)
    all_states = scan_blocks(segment_starts, all_fresh, decay)
    states = lax.all_to_all(all_states, "seq", 0, 0, tiled=True)
    gated = gate(entering, query, base, states)
    behind, ahead, across = (shifted(gated, "fsdp", by) for by in (1, 3, 2))
    total = project((0, 2), [gated, across], weight, None, F32)
    total = project((3,), [behind], weight, total, F32)
    return project((1,), [ahead], weight, total, BF16)


def solution(mesh):
    return jax.shard_map(
        on_device,
        mesh=mesh,
        in_specs=(
            P(("dp", "seq"), None, "fsdp"),
            P(None, None, "fsdp"),
            P("fsdp", None),
            P("fsdp", None),
            P("fsdp"),
            P("dp"),
            P("seq", "fsdp"),
        ),
        out_specs=P(("dp", "seq"), "fsdp"),
        check_vma=False,
    )
```
